256 devices in a mesh: grp: 8 (over y, z_lo), dev: 32 (over z_hi, x, core).
Axes of the slice: x: 4, y: 4, z: 8 (z_hi: 4, z_lo: 2; z = z_hi * 2 + z_lo), core: 2. Of those that a mesh axis runs over, the one named last changes fastest.
Arguments:
- reservoir: bfloat16 [262144, 1024], P(('grp', 'dev')), may hold values from -6 to 6
- send_rows: int32 [256, 8, 16], P(('grp', 'dev')), may hold values from 0 to 1023
- send_count: int32 [256, 8], P(('grp', 'dev')), may hold values from 0 to 16, as said below
- new_rows: bfloat16 [131072, 1024], P(('grp', 'dev')), may hold values from -6 to 6
- w_up: bfloat16 [1024, 2048], P('dev'), may hold values from -0.1875 to 0.1875
- w_down: bfloat16 [2048, 1024], P('dev'), may hold values from -0.125 to 0.125
- ln_gain: bfloat16 [1024], replicated, may hold values from 0.099609375 to 1.8984375
- grad_new: bfloat16 [131072, 1024], P(('grp', 'dev')), may hold values from -0.016479492 to 0.016479492
- grad_old: bfloat16 [32768, 1024], P(('grp', 'dev')), may hold values from -0.016479492 to 0.016479492
Outputs:
- block_out: bfloat16 [131072, 1024], P(('grp', 'dev'))
- grad_up: float32 [1024, 2048], P('dev')
- grad_down: float32 [2048, 1024], P('dev')
The draws below stay inside these ranges and needn't reach their ends.
Inputs may be any that keep to these rules, and one draw needn't show every extreme that they name: send_count[s, t] slots of source s toward group t are live, the others are empty; 16 is reached in every draw, and about a quarter of the (source, group) pairs carry 8 to 16 live slots, the others 0 to 4.
All inputs are finite; a program needn't handle non-finite values.
Results may differ from the reference program's by a relative error of at most 0.024.
Values may be sent and summed in bfloat16 or wider, within the bound.
No kernel may reach another device: no remote copies, remote signals or barrier semaphores. Data moves between devices by JAX's collectives and lax.ppermute only.
A program may use at most 64 MiB of HBM per device.

```python
import jax
import jax.numpy as jnp
from jax import lax

D = 1024
HID = 2048
NEW_DEV = 512
CAP = 16
RES_DEV = 1024
TOKENS = 131072
STORED = 262144
OLD = 32768
N_GRP = 8
N_DEV = 32


def draw_send_count(key, part):
    key = jax.random.fold_in(key, 11)
    keys = jax.random.split(key, 4)
    shape = (N_GRP * N_DEV, N_GRP)
    heavy = jax.random.randint(keys[0], shape, 0, 4) == 0
    light_counts = jax.random.randint(keys[1], shape, 0, CAP // 4 + 1)
    heavy_counts = jax.random.randint(keys[2], shape, CAP // 2, CAP + 1)
    counts = jnp.where(heavy, heavy_counts, light_counts).reshape(-1)
    spot = jax.random.randint(keys[3], (), 0, N_GRP * N_DEV * N_GRP)
    counts = counts.at[spot].set(CAP)
    return counts.reshape(shape).astype(jnp.int32)


def plant(result, own_key, smallest, top_value):
    dims = result.shape
    index_at = [jax.random.randint(jax.random.fold_in(own_key, axis), (), 0, dims[axis]) for axis in range(len(dims))]
    result = result.at[tuple(index_at)].set(smallest)
    longest = dims.index(max(dims))
    index_at[longest] = (index_at[longest] + 1) % dims[longest]
    return result.at[tuple(index_at)].set(top_value)


def steps_of(rng, dims, cuts, least, high):
    gain = 1.0
    for position, blocks in cuts:
        steps = jax.random.uniform(jax.random.fold_in(jax.random.fold_in(rng, 6), position), (blocks,), jnp.float32, least / len(cuts), high / len(cuts))
        gain = gain * jnp.repeat(jnp.exp(steps), dims[position] // blocks).reshape((-1,) + (1,) * (len(dims) - 1 - position))
    return gain


def gaussian(own_key, dims, width, limit, shards=(), held_as=jnp.bfloat16):
    level = steps_of(own_key, dims, shards, -0.22, 0.18) if shards else 1.0
    result = jax.random.normal(own_key, dims, jnp.float32) * width * level
    return jnp.minimum(jnp.maximum(result, -limit), limit).astype(held_as)


def setup_inputs(seed: int = 0) -> dict:
    key_of = jax.random.split(jax.random.key(seed), 10)
    reservoir = gaussian(key_of[0], (STORED, D), 1.0, 6.0, ((0, 256),))
    send_rows = plant(jax.random.randint(key_of[1], (N_GRP * N_DEV, N_GRP, CAP), 0, RES_DEV), jax.random.fold_in(key_of[1], 1), 0, RES_DEV - 1).astype(jnp.int32)
    send_count = draw_send_count(jax.random.fold_in(key_of[9], 71), 0)
    new_rows = gaussian(key_of[3], (TOKENS, D), 1.0, 6.0, ((0, 256),))
    w_up = gaussian(key_of[4], (D, HID), D ** -0.5, 0.1875, ((0, 32),))
    w_down = gaussian(key_of[5], (HID, D), HID ** -0.5, 0.125, ((0, 32),))
    ln_gain = jnp.clip(1.0 + 0.18 * jax.random.normal(key_of[6], (D,), jnp.float32), 0.099609375, 1.8984375).astype(jnp.bfloat16)
    grad_new = gaussian(key_of[7], (TOKENS, D), (1.0 / (N_GRP * N_DEV * NEW_DEV) ** 0.5), 0.016479492, ((0, 256),))
    grad_old = gaussian(key_of[8], (OLD, D), (1.0 / (N_GRP * N_DEV * NEW_DEV) ** 0.5), 0.016479492, ((0, 256),))
    return {"reservoir": reservoir, "send_rows": send_rows, "send_count": send_count, "new_rows": new_rows, "w_up": w_up, "w_down": w_down, "ln_gain": ln_gain, "grad_new": grad_new, "grad_old": grad_old}


def normalize(rows, ln_gain):
    values = rows.astype(jnp.float32)
    center = lax.optimization_barrier(jnp.mean(values, axis=-1, keepdims=True))
    centred = values - center
    spread = lax.optimization_barrier(jnp.mean(centred * centred, axis=-1, keepdims=True))
    return (centred * lax.rsqrt(spread + 1e-05) * ln_gain.astype(jnp.float32)).astype(jnp.bfloat16)

def gelu_parts(pre):
    cdf_value = 0.5 * (1.0 + lax.erf(pre * 0.7071067811865476))
    density = jnp.exp(-0.5 * pre * pre) * 0.3989422804014327
    return (pre * cdf_value, cdf_value + pre * density)

def reference(reservoir, send_rows, send_count, new_rows, w_up, w_down, ln_gain, grad_new, grad_old):
    slot_ids = jnp.arange(CAP, dtype=jnp.int32)
    group_ids = jnp.arange(N_GRP, dtype=jnp.int32)
    old_block = N_GRP * CAP

    def per_device(carry, device):
        target = device // N_DEV
        lane = device % N_DEV
        sources = group_ids * N_DEV + lane
        picks = send_rows[sources, target]
        counts = send_count[sources, target]
        where_rows = (sources[:, None] * RES_DEV + picks).reshape(-1).astype(jnp.int32)
        live = (slot_ids[None, :] < counts[:, None]).astype(jnp.bfloat16).reshape(-1, 1)
        old = reservoir[where_rows] * live
        fresh = lax.dynamic_slice_in_dim(new_rows, (device * NEW_DEV).astype(jnp.int32), NEW_DEV, 0)
        rows = jnp.concatenate([fresh, old], axis=0)
        normed = normalize(rows, ln_gain)
        pre = jnp.dot(normed, w_up, preferred_element_type=jnp.float32)
        act, slope = gelu_parts(pre)
        hidden = act.astype(jnp.bfloat16)
        mixed = jnp.dot(hidden[:NEW_DEV], w_down, preferred_element_type=jnp.float32)
        out_rows = (fresh.astype(jnp.float32) + mixed).astype(jnp.bfloat16)
        cot_new = lax.dynamic_slice_in_dim(grad_new, (device * NEW_DEV).astype(jnp.int32), NEW_DEV, 0)
        cot_old = lax.dynamic_slice_in_dim(grad_old, (device * old_block).astype(jnp.int32), old_block, 0)
        cot = jnp.concatenate([cot_new, cot_old], axis=0)
        back = lax.dot_general(cot, w_down, (((1,), (1,)), ((), ())), preferred_element_type=jnp.float32)
        pre_grad = (back * slope).astype(jnp.bfloat16)
        term_down = lax.dot_general(hidden, cot, (((0,), (0,)), ((), ())), preferred_element_type=jnp.float32)
        term_up = lax.dot_general(normed, pre_grad, (((0,), (0,)), ((), ())), preferred_element_type=jnp.float32)
        term_down = lax.optimization_barrier(term_down.astype(jnp.bfloat16)).astype(jnp.float32)
        term_up = lax.optimization_barrier(term_up.astype(jnp.bfloat16)).astype(jnp.float32)
        return ((carry[0] + term_up, carry[1] + term_down), out_rows)
    start = (jnp.zeros((D, HID), jnp.float32), jnp.zeros((HID, D), jnp.float32))
    devices = jnp.arange(N_GRP * N_DEV, dtype=jnp.int32)
    (grad_up, grad_down), outs = lax.scan(per_device, start, devices)
    return (outs.reshape(N_GRP * N_DEV * NEW_DEV, D), grad_up, grad_down)
```

```python
import jax
import jax.numpy as jnp
from jax import lax
from jax.sharding import Mesh, PartitionSpec as P

PHYSICAL = (("y", 4), ("zl", 2), ("zh", 4), ("x", 4), ("c", 2))
AXES = tuple(name for name, _ in PHYSICAL)
GRP = ("y", "zl")
DEV = ("zh", "x", "c")


def normalize(rows, ln_gain):
    values = rows.astype(jnp.float32)
    center = jnp.mean(values, axis=-1, keepdims=True)
    centred = values - center
    spread = jnp.mean(centred * centred, axis=-1, keepdims=True)
    return (centred * lax.rsqrt(spread + 1e-05) * ln_gain.astype(jnp.float32)).astype(jnp.bfloat16)


def gelu_parts(pre):
    cdf_value = 0.5 * (1.0 + lax.erf(pre * 0.7071067811865476))
    density = jnp.exp(-0.5 * pre * pre) * 0.3989422804014327
    return (pre * cdf_value, cdf_value + pre * density)


def swap(value):
    return lax.ppermute(value, "c", [(0, 1), (1, 0)])


def exchange(value, axes):
    return lax.all_to_all(value, axes, split_axis=0, concat_axis=0, tiled=True)


def gather_zh(value):
    n = lax.axis_size("zh")
    parts = [value]
    for step in range(1, n):
        parts.append(lax.ppermute(value, "zh", [((i + step) % n, i) for i in range(n)]))
    ring = jnp.stack(parts + parts[:-1])
    return lax.dynamic_slice_in_dim(ring, (n - lax.axis_index("zh")) % n, n, 0)


def body(reservoir, send_rows, send_count, new_rows, w_up, w_down, ln_gain, grad_new, grad_old):
    n_grp, n_zh, n_x, n_c = lax.axis_size(GRP), lax.axis_size("zh"), lax.axis_size("x"), lax.axis_size("c")
    slots = send_rows.shape[2]
    fresh_count, width = new_rows.shape
    up_rows, hid = w_up.shape
    down_rows = w_down.shape[0]
    half = hid // n_c
    cut = half // n_grp
    pair = cut // down_rows
    group = lax.axis_index(GRP)

    mine = lax.dynamic_index_in_dim(w_up.reshape(up_rows, n_grp, pair, n_c, down_rows), group, 1, keepdims=False)
    mine = mine.transpose(2, 0, 1, 3).reshape(n_c, up_rows, cut)
    column = gather_zh(mine).transpose(1, 0, 2, 3)
    spread_up = jnp.broadcast_to(column[None], (n_grp * n_x,) + column.shape)
    spread_up = spread_up.reshape(n_grp * n_x * n_c, n_zh, up_rows, cut)

    live = (lax.broadcasted_iota(jnp.int32, (n_grp, slots), 1) < send_count[0][:, None]).astype(jnp.bfloat16)
    picked = reservoir[send_rows[0].reshape(-1)].reshape(n_grp, slots, width) * live[:, :, None]
    arrived = exchange(picked, GRP).reshape(n_grp * slots, width)

    down_half = lax.all_gather(w_down, ("zh", "x"), axis=0, tiled=True)
    got_up = exchange(spread_up, ("y", "zl", "x", "c")).reshape(n_grp, n_x, n_c, n_zh, up_rows, cut)
    up_half = got_up.transpose(3, 1, 2, 4, 0, 5).reshape(width, half)

    normed_own = normalize(jnp.concatenate([new_rows, arrived], axis=0), ln_gain)
    cot_own = jnp.concatenate([grad_new, grad_old], axis=0)
    normed = jnp.concatenate([normed_own, swap(normed_own)], axis=0)
    cot = jnp.concatenate([cot_own, swap(cot_own)], axis=0)
    rows = normed_own.shape[0]

    pre = jnp.dot(normed, up_half, preferred_element_type=jnp.float32)
    act, slope = gelu_parts(pre)
    hidden = act.astype(jnp.bfloat16)

    term_down = lax.dot_general(hidden, cot, (((0,), (0,)), ((), ())), preferred_element_type=jnp.float32)
    term_down = term_down.astype(jnp.bfloat16).reshape(n_zh, n_x, down_rows, n_grp, cut)
    term_down = term_down.transpose(3, 1, 0, 2, 4).reshape(n_grp * n_x, n_zh, down_rows, cut)
    part_down = jnp.sum(exchange(term_down, ("y", "zl", "x")).astype(jnp.float32), axis=0).astype(jnp.bfloat16)

    back = lax.dot_general(cot, down_half, (((1,), (1,)), ((), ())), preferred_element_type=jnp.float32)
    pre_grad = (back * slope).astype(jnp.bfloat16)
    term_up = lax.dot_general(normed, pre_grad, (((0,), (0,)), ((), ())), preferred_element_type=jnp.float32)
    term_up = term_up.astype(jnp.bfloat16).reshape(n_zh, n_x, n_c, up_rows, n_grp, cut)
    term_up = term_up.transpose(4, 1, 2, 0, 3, 5).reshape(n_grp * n_x * n_c, n_zh, up_rows, cut)
    part_up = exchange(term_up, ("y", "zl", "x", "c")).reshape(n_grp * n_x, n_c, n_zh, up_rows, cut)
    part_up = jnp.sum(part_up.astype(jnp.float32), axis=0).astype(jnp.bfloat16)

    other = jnp.dot(hidden[rows : rows + fresh_count], down_half, preferred_element_type=jnp.float32)
    mixed = jnp.dot(hidden[:fresh_count], down_half, preferred_element_type=jnp.float32)
    returned = swap(other.astype(jnp.bfloat16)).astype(jnp.float32)
    block_out = (new_rows.astype(jnp.float32) + (mixed + returned)).astype(jnp.bfloat16)

    both = jnp.concatenate([part_down[:, None], part_up.transpose(1, 0, 2, 3).reshape(n_zh, 1, n_c * up_rows, cut)], axis=1)
    both = jnp.broadcast_to(both[:, None], (n_zh, n_grp) + both.shape[1:]).reshape((n_zh * n_grp,) + both.shape[1:])
    both = exchange(both, ("zh", "y", "zl")).reshape((n_zh, n_grp) + both.shape[1:])
    both = jnp.sum(both.astype(jnp.float32), axis=0)
    grad_down = both[:, 0].transpose(1, 0, 2).reshape(down_rows, width)
    grad_up = both[:, 1].reshape(n_grp, n_c, up_rows, pair, down_rows)
    grad_up = grad_up.transpose(2, 0, 3, 1, 4).reshape(up_rows, hid)
    return (block_out, grad_up, grad_down)


def solution(mesh):
    fine = Mesh(mesh.devices.reshape(tuple(size for _, size in PHYSICAL)), AXES)
    every = P(AXES, None)
    return jax.shard_map(
        body,
        mesh=fine,
        in_specs=(every, P(AXES, None, None), every, every, P(DEV, None), P(DEV, None), P(), every, every),
        out_specs=(every, P(DEV, None), P(DEV, None)),
        check_vma=False,
    )
```

```python
import jax
import jax.numpy as jnp
from jax import lax
from jax.experimental import pallas as pl
from jax.experimental.pallas import tpu as pltpu
from jax.sharding import Mesh, PartitionSpec as P

PHYSICAL = (("y", 4), ("zl", 2), ("zh", 4), ("x", 4), ("c", 2))
SIZE = dict(PHYSICAL)
AXES = tuple(name for name, _ in PHYSICAL)
GRP = ("y", "zl")
DEV = ("zh", "x", "c")
N_GRP = SIZE["y"] * SIZE["zl"]
N_ZH, N_X, N_C = SIZE["zh"], SIZE["x"], SIZE["c"]
VMEM_BYTES = 48 * 1024 * 1024


def normalize(rows, ln_gain):
    values = rows.astype(jnp.float32)
    center = jnp.mean(values, axis=-1, keepdims=True)
    centred = values - center
    spread = jnp.mean(centred * centred, axis=-1, keepdims=True)
    return (centred * lax.rsqrt(spread + 1e-05) * ln_gain.astype(jnp.float32)).astype(jnp.bfloat16)


def gelu_parts(pre):
    cdf_value = 0.5 * (1.0 + lax.erf(pre * 0.7071067811865476))
    density = jnp.exp(-0.5 * pre * pre) * 0.3989422804014327
    return (pre * cdf_value, cdf_value + pre * density)


def swap(value):
    return lax.ppermute(value, "c", [(0, 1), (1, 0)])


def exchange(value, axes):
    return lax.all_to_all(value, axes, split_axis=0, concat_axis=0, tiled=True)


def shift_zh(value, step):
    return lax.ppermute(value, "zh", [(i, (i + step) % N_ZH) for i in range(N_ZH)])


def lanes_split(left, right):
    low = lax.broadcasted_iota(jnp.int32, left.shape, 1) < 64
    first = jnp.where(low, left, pltpu.roll(right, 64, 1))
    second = jnp.where(low, pltpu.roll(left, 64, 1), right)
    return first, second


def cut_kernel(group_ref, w_ref, out_ref):
    value = w_ref[...].astype(jnp.float32)
    first, second = lanes_split(value[:, :128], value[:, 128:])
    out_ref[0] = first.astype(out_ref.dtype)
    out_ref[1] = second.astype(out_ref.dtype)


def cut_up(w_up, group):
    rows = w_up.shape[0]
    return pl.pallas_call(
        cut_kernel,
        grid_spec=pltpu.PrefetchScalarGridSpec(
            num_scalar_prefetch=1,
            grid=(1,),
            in_specs=[pl.BlockSpec((rows, 256), lambda i, g: (0, g[0]))],
            out_specs=pl.BlockSpec((2, rows, 128), lambda i, g: (0, 0, 0)),
        ),
        out_shape=jax.ShapeDtypeStruct((2, rows, 128), w_up.dtype),
        name="cut_up",
    )(group.reshape(1), w_up)


def final_kernel(both_ref, down_ref, up_ref):
    rows = up_ref.shape[0]
    for g in range(N_GRP):
        down_ref[:, g * 128 : (g + 1) * 128] = both_ref[g, 0].astype(jnp.float32)
        left = both_ref[g, 1, :rows].astype(jnp.float32)
        right = both_ref[g, 1, rows:].astype(jnp.float32)
        first, second = lanes_split(left, right)
        up_ref[:, g * 256 : g * 256 + 128] = first
        up_ref[:, g * 256 + 128 : g * 256 + 256] = second


def finish(both, width, hid):
    rows = both.shape[2]
    return pl.pallas_call(
        final_kernel,
        out_shape=(
            jax.ShapeDtypeStruct((rows, width), jnp.float32),
            jax.ShapeDtypeStruct((rows // N_C, hid), jnp.float32),
        ),
        name="finish",
    )(both)


def join_cot(parts, cot):
    at = 0
    for part in parts:
        cot[at : at + part.shape[0], :] = part[...]
        at += part.shape[0]


def forward_kernel(zh_ref, own_ref, partner_ref, c0, c1, c2, c3, w_ref, hidden_ref, slope_ref, term_ref, w, cot):
    @pl.when(pl.program_id(0) == 0)
    def _():
        join_cot((c0, c1, c2, c3), cot)

    for j in range(N_ZH):
        at = pl.multiple_of(((zh_ref[0] + j) % N_ZH) * 256, 256)
        for g in range(2):
            w[pl.ds(at, 256), g * 128 : (g + 1) * 128] = w_ref[g, :, :, j].reshape(256, 128)
    rows = own_ref.shape[0]
    step = rows // 2
    for which, ref in enumerate((own_ref, partner_ref)):
        for at in range(0, rows, step):
            pre = jnp.dot(ref[at : at + step, :], w[...], preferred_element_type=jnp.float32)
            act, slope = gelu_parts(pre)
            to = which * rows + at
            hidden_ref[to : to + step, :] = act.astype(jnp.bfloat16)
            slope_ref[to : to + step, :] = slope.astype(jnp.bfloat16)
    term = lax.dot_general(hidden_ref[...], cot[...], (((0,), (0,)), ((), ())), preferred_element_type=jnp.float32)
    term = term.astype(jnp.bfloat16)
    for x in range(N_X):
        for g in range(N_GRP):
            term_ref[g, x, 0] = term[x * 64 : (x + 1) * 64, g * 128 : (g + 1) * 128]


def whole(array):
    return pl.BlockSpec(array.shape, lambda *i: (0,) * array.ndim)


def forward(zh, own, partner, cots, got_up):
    rows, width = own.shape
    half = N_GRP * 128
    return pl.pallas_call(
        forward_kernel,
        grid_spec=pltpu.PrefetchScalarGridSpec(
            num_scalar_prefetch=1,
            grid=(N_ZH,),
            in_specs=[
                whole(own),
                whole(partner),
                *[whole(c) for c in cots],
                pl.BlockSpec((2,) + got_up.shape[1:], lambda q, z: (q, 0, 0, 0, 0, 0)),
            ],
            out_specs=[
                pl.BlockSpec((2 * rows, 256), lambda q, z: (0, q)),
                pl.BlockSpec((2 * rows, 256), lambda q, z: (0, q)),
                pl.BlockSpec((N_GRP, N_X, 1, 64, 128), lambda q, z: (0, 0, q, 0, 0)),
            ],
            scratch_shapes=[pltpu.VMEM((width, 256), jnp.bfloat16), pltpu.VMEM((2 * rows, width), jnp.bfloat16)],
        ),
        out_shape=(
            jax.ShapeDtypeStruct((2 * rows, half), jnp.bfloat16),
            jax.ShapeDtypeStruct((2 * rows, half), jnp.bfloat16),
            jax.ShapeDtypeStruct((N_GRP, N_X, N_ZH, 64, 128), jnp.bfloat16),
        ),
        compiler_params=pltpu.CompilerParams(vmem_limit_bytes=VMEM_BYTES),
        cost_estimate=pl.CostEstimate(
            flops=8 * rows * width * half, bytes_accessed=24 * 1024 * 1024, transcendentals=4 * rows * half
        ),
        name="forward",
    )(zh.reshape(1), own, partner, *cots, got_up)


def backward_kernel(own_ref, partner_ref, c0, c1, c2, c3, w_ref, slope_ref, term_ref, pre_grad, cot):
    @pl.when(pl.program_id(0) == 0)
    def _():
        join_cot((c0, c1, c2, c3), cot)

    rows = own_ref.shape[0]
    step = rows // 2
    for at in range(0, 2 * rows, step):
        back = lax.dot_general(
            cot[at : at + step, :], w_ref[...], (((1,), (1,)), ((), ())), preferred_element_type=jnp.float32
        )
        slope = slope_ref[at : at + step, :].astype(jnp.float32)
        pre_grad[at : at + step, :] = (back * slope).astype(jnp.bfloat16)
    dims = (((0,), (0,)), ((), ()))
    term = lax.dot_general(own_ref[...], pre_grad[:rows, :], dims, preferred_element_type=jnp.float32)
    term += lax.dot_general(partner_ref[...], pre_grad[rows:, :], dims, preferred_element_type=jnp.float32)
    term = term.astype(jnp.bfloat16)
    for g in range(2):
        for z in range(N_ZH):
            for x in range(N_X):
                for c in range(N_C):
                    at = z * 256 + x * 64 + c * 32
                    term_ref[g, x, c, z] = term[at : at + 32, g * 128 : (g + 1) * 128]


def backward(own, partner, cots, down_half, slope):
    rows, width = own.shape
    half = down_half.shape[0]
    return pl.pallas_call(
        backward_kernel,
        grid=(half // 256,),
        in_specs=[
            whole(own),
            whole(partner),
            *[whole(c) for c in cots],
            pl.BlockSpec((256, width), lambda q: (q, 0)),
            pl.BlockSpec((2 * rows, 256), lambda q: (0, q)),
        ],
        out_specs=pl.BlockSpec((2, N_X, N_C, N_ZH, 32, 128), lambda q: (q, 0, 0, 0, 0, 0)),
        out_shape=jax.ShapeDtypeStruct((N_GRP, N_X, N_C, N_ZH, 32, 128), jnp.bfloat16),
        scratch_shapes=[pltpu.VMEM((2 * rows, 256), jnp.bfloat16), pltpu.VMEM((2 * rows, width), jnp.bfloat16)],
        compiler_params=pltpu.CompilerParams(vmem_limit_bytes=VMEM_BYTES),
        cost_estimate=pl.CostEstimate(
            flops=8 * rows * width * half, bytes_accessed=20 * 1024 * 1024, transcendentals=0
        ),
        name="backward",
    )(own, partner, *cots, down_half, slope)


def sum_zh(part, zh):
    total = lax.dynamic_index_in_dim(part, zh, 0, keepdims=False).astype(jnp.float32)
    for step in range(1, N_ZH):
        block = lax.dynamic_index_in_dim(part, (zh + step) % N_ZH, 0, keepdims=False)
        total += shift_zh(block, step).astype(jnp.float32)
    return total.astype(jnp.bfloat16)


def body(reservoir, send_rows, send_count, new_rows, w_up, w_down, ln_gain, grad_new, grad_old):
    slots = send_rows.shape[2]
    fresh_count, width = new_rows.shape
    up_rows, hid = w_up.shape
    group, zh = lax.axis_index(GRP), lax.axis_index("zh")

    down_half = lax.all_gather(w_down, ("zh", "x"), axis=0, tiled=True)

    mine = cut_up(w_up, group)
    column = jnp.stack([mine] + [shift_zh(mine, -step) for step in range(1, N_ZH)], axis=1)
    spread_up = jnp.broadcast_to(column[None], (N_GRP * N_X,) + column.shape)
    spread_up = spread_up.reshape(N_GRP * N_X * N_C, N_ZH, up_rows, 128)
    got_up = exchange(spread_up, ("y", "zl", "x", "c")).reshape(N_GRP, N_X, N_C, N_ZH, up_rows, 128)

    grad_new, grad_old, _ = lax.optimization_barrier((grad_new, grad_old, spread_up))
    blocks = grad_old.reshape(N_GRP, slots, width)
    y, zl = group // SIZE["zl"], group % SIZE["zl"]
    order, old_cot = [], []
    for dy in range(SIZE["y"]):
        for dz in range(SIZE["zl"]):
            to = (y + dy) % SIZE["y"] * SIZE["zl"] + (zl + dz) % SIZE["zl"]
            order.append((y - dy) % SIZE["y"] * SIZE["zl"] + (zl + dz) % SIZE["zl"])
            block = lax.dynamic_index_in_dim(blocks, to, 0, keepdims=False)
            if dy or dz:
                perm = [
                    (a * 2 + b, (a + dy) % SIZE["y"] * 2 + (b + dz) % 2)
                    for a in range(SIZE["y"])
                    for b in range(SIZE["zl"])
                ]
                block = lax.ppermute(block, GRP, perm)
            old_cot.append(block)
    old_cot = jnp.concatenate(old_cot, axis=0)
    order = jnp.stack(order)
    picks, counts = send_rows[0][order], send_count[0][order]
    live = (lax.broadcasted_iota(jnp.int32, (N_GRP, slots), 1) < counts[:, None]).astype(jnp.bfloat16)
    picked = reservoir[picks.reshape(-1)] * live.reshape(-1, 1)

    normed = normalize(jnp.concatenate([new_rows, picked], axis=0), ln_gain)
    partner = swap(normed)
    cots = (grad_new, old_cot, swap(grad_new), swap(old_cot))
    rows = normed.shape[0]

    hidden, slope, term_down = forward(zh, normed, partner, cots, got_up)
    part_down = exchange(term_down.reshape(N_GRP * N_X, N_ZH, 64, 128), ("y", "zl", "x"))
    part_down = jnp.sum(part_down.astype(jnp.float32), axis=0).astype(jnp.bfloat16)
    sum_down = sum_zh(part_down, zh)

    term_up = backward(normed, partner, cots, down_half, slope)
    part_up = exchange(term_up.reshape(N_GRP * N_X * N_C, N_ZH, up_rows, 128), ("y", "zl", "x", "c"))
    part_up = part_up.reshape(N_GRP * N_X, N_C, N_ZH, up_rows, 128)
    part_up = jnp.sum(part_up.astype(jnp.float32), axis=0).astype(jnp.bfloat16)
    sum_up = sum_zh(part_up.transpose(1, 0, 2, 3).reshape(N_ZH, N_C * up_rows, 128), zh)

    other = jnp.dot(hidden[rows : rows + fresh_count], down_half, preferred_element_type=jnp.float32)
    mixed = jnp.dot(hidden[:fresh_count], down_half, preferred_element_type=jnp.float32)
    returned = swap(other.astype(jnp.bfloat16)).astype(jnp.float32)
    block_out = (new_rows.astype(jnp.float32) + (mixed + returned)).astype(jnp.bfloat16)

    both = jnp.stack([sum_down, sum_up])
    both = exchange(jnp.broadcast_to(both[None], (N_GRP,) + both.shape), GRP)
    grad_down, grad_up = finish(both, width, hid)
    return (block_out, grad_up, grad_down)


def solution(mesh):
    fine = Mesh(mesh.devices.reshape(tuple(size for _, size in PHYSICAL)), AXES)
    every = P(AXES, None)
    return jax.shard_map(
        body,
        mesh=fine,
        in_specs=(every, P(AXES, None, None), every, every, P(DEV, None), P(DEV, None), P(), every, every),
        out_specs=(every, P(DEV, None), P(DEV, None)),
        check_vma=False,
    )
```

```python
import jax
import jax.numpy as jnp
from jax import lax
from jax.experimental import pallas as pl
from jax.experimental.pallas import tpu as pltpu
from jax.sharding import Mesh, PartitionSpec as P

PHYSICAL = (("y", 4), ("zl", 2), ("zh", 4), ("x", 4), ("c", 2))
SIZE = dict(PHYSICAL)
AXES = tuple(name for name, _ in PHYSICAL)
GRP = ("y", "zl")
DEV = ("zh", "x", "c")
N_GRP = SIZE["y"] * SIZE["zl"]
N_ZH, N_X, N_C = SIZE["zh"], SIZE["x"], SIZE["c"]
VMEM_BYTES = 48 * 1024 * 1024


def normalize(rows, ln_gain):
    values = rows.astype(jnp.float32)
    center = jnp.mean(values, axis=-1, keepdims=True)
    centred = values - center
    spread = jnp.mean(centred * centred, axis=-1, keepdims=True)
    return (centred * lax.rsqrt(spread + 1e-05) * ln_gain.astype(jnp.float32)).astype(jnp.bfloat16)


def gelu_parts(pre):
    cdf_value = 0.5 * (1.0 + lax.erf(pre * 0.7071067811865476))
    density = jnp.exp(-0.5 * pre * pre) * 0.3989422804014327
    return (pre * cdf_value, cdf_value + pre * density)


def swap(value):
    return lax.ppermute(value, "c", [(0, 1), (1, 0)])


def exchange(value, axes):
    return lax.all_to_all(value, axes, split_axis=0, concat_axis=0, tiled=True)


def shift_zh(value, step):
    return lax.ppermute(value, "zh", [(i, (i + step) % N_ZH) for i in range(N_ZH)])


def lanes_split(left, right):
    low = lax.broadcasted_iota(jnp.int32, left.shape, 1) < 64
    first = jnp.where(low, left, pltpu.roll(right, 64, 1))
    second = jnp.where(low, pltpu.roll(left, 64, 1), right)
    return first, second


def cut_kernel(group_ref, w_ref, out_ref):
    value = w_ref[...].astype(jnp.float32)
    first, second = lanes_split(value[:, :128], value[:, 128:])
    out_ref[0] = first.astype(out_ref.dtype)
    out_ref[1] = second.astype(out_ref.dtype)


def cut_up(w_up, group):
    rows = w_up.shape[0]
    return pl.pallas_call(
        cut_kernel,
        grid_spec=pltpu.PrefetchScalarGridSpec(
            num_scalar_prefetch=1,
            grid=(1,),
            in_specs=[pl.BlockSpec((rows, 256), lambda i, g: (0, g[0]))],
            out_specs=pl.BlockSpec((2, rows, 128), lambda i, g: (0, 0, 0)),
        ),
        out_shape=jax.ShapeDtypeStruct((2, rows, 128), w_up.dtype),
        name="cut_up",
    )(group.reshape(1), w_up)


def final_kernel(both_ref, down_ref, up_ref):
    rows = up_ref.shape[0]
    for g in range(N_GRP):
        down_ref[:, g * 128 : (g + 1) * 128] = both_ref[g, 0].astype(jnp.float32)
        left = both_ref[g, 1, :rows].astype(jnp.float32)
        right = both_ref[g, 1, rows:].astype(jnp.float32)
        first, second = lanes_split(left, right)
        up_ref[:, g * 256 : g * 256 + 128] = first
        up_ref[:, g * 256 + 128 : g * 256 + 256] = second


def finish(both, width, hid):
    rows = both.shape[2]
    return pl.pallas_call(
        final_kernel,
        out_shape=(
            jax.ShapeDtypeStruct((rows, width), jnp.float32),
            jax.ShapeDtypeStruct((rows // N_C, hid), jnp.float32),
        ),
        name="finish",
    )(both)


def join_cot(parts, cot):
    at = 0
    for part in parts:
        cot[at : at + part.shape[0], :] = part[...]
        at += part.shape[0]


def forward_kernel(zh_ref, own_ref, partner_ref, c0, c1, c2, c3, w_ref, hidden_ref, slope_ref, term_ref, w, cot):
    @pl.when(pl.program_id(0) == 0)
    def _():
        join_cot((c0, c1, c2, c3), cot)

    for j in range(N_ZH):
        at = pl.multiple_of(((zh_ref[0] + j) % N_ZH) * 256, 256)
        for g in range(2):
            w[pl.ds(at, 256), g * 128 : (g + 1) * 128] = w_ref[g, :, :, j].reshape(256, 128)
    rows = own_ref.shape[0]
    step = rows // 2
    for which, ref in enumerate((own_ref, partner_ref)):
        for at in range(0, rows, step):
            pre = jnp.dot(ref[at : at + step, :], w[...], preferred_element_type=jnp.float32)
            act, slope = gelu_parts(pre)
            to = which * rows + at
            hidden_ref[to : to + step, :] = act.astype(jnp.bfloat16)
            slope_ref[to : to + step, :] = slope.astype(jnp.bfloat16)
    term = lax.dot_general(hidden_ref[...], cot[...], (((0,), (0,)), ((), ())), preferred_element_type=jnp.float32)
    term = term.astype(jnp.bfloat16)
    for x in range(N_X):
        for g in range(N_GRP):
            term_ref[g, x, 0] = term[x * 64 : (x + 1) * 64, g * 128 : (g + 1) * 128]


def whole(array):
    return pl.BlockSpec(array.shape, lambda *i: (0,) * array.ndim)


def forward(zh, own, partner, cots, got_up):
    rows, width = own.shape
    half = N_GRP * 128
    return pl.pallas_call(
        forward_kernel,
        grid_spec=pltpu.PrefetchScalarGridSpec(
            num_scalar_prefetch=1,
            grid=(N_ZH,),
            in_specs=[
                whole(own),
                whole(partner),
                *[whole(c) for c in cots],
                pl.BlockSpec((2,) + got_up.shape[1:], lambda q, z: (q, 0, 0, 0, 0, 0)),
            ],
            out_specs=[
                pl.BlockSpec((2 * rows, 256), lambda q, z: (0, q)),
                pl.BlockSpec((2 * rows, 256), lambda q, z: (0, q)),
                pl.BlockSpec((N_GRP, N_X, 1, 64, 128), lambda q, z: (0, 0, q, 0, 0)),
            ],
            scratch_shapes=[pltpu.VMEM((width, 256), jnp.bfloat16), pltpu.VMEM((2 * rows, width), jnp.bfloat16)],
        ),
        out_shape=(
            jax.ShapeDtypeStruct((2 * rows, half), jnp.bfloat16),
            jax.ShapeDtypeStruct((2 * rows, half), jnp.bfloat16),
            jax.ShapeDtypeStruct((N_GRP, N_X, N_ZH, 64, 128), jnp.bfloat16),
        ),
        compiler_params=pltpu.CompilerParams(vmem_limit_bytes=VMEM_BYTES),
        cost_estimate=pl.CostEstimate(
            flops=0, bytes_accessed=1024, transcendentals=0
        ),
        name="forward",
    )(zh.reshape(1), own, partner, *cots, got_up)


def backward_kernel(core_ref, own_ref, partner_ref, c0, c1, c2, c3, w_ref, slope_ref, term_ref, pre_grad, cot):
    @pl.when(pl.program_id(0) == 0)
    def _():
        join_cot((c0, c1, c2, c3), cot)

    rows, width = own_ref.shape
    step = rows // 2
    w = w_ref[...].reshape(256, width)
    for at in range(0, 2 * rows, step):
        back = lax.dot_general(
            cot[at : at + step, :], w, (((1,), (1,)), ((), ())), preferred_element_type=jnp.float32
        )
        slope = slope_ref[at : at + step, :].astype(jnp.float32)
        pre_grad[at : at + step, :] = (back * slope).astype(jnp.bfloat16)
    dims = (((0,), (0,)), ((), ()))
    term = lax.dot_general(own_ref[...], pre_grad[:rows, :], dims, preferred_element_type=jnp.float32)
    term += lax.dot_general(partner_ref[...], pre_grad[rows:, :], dims, preferred_element_type=jnp.float32)
    term = term.astype(jnp.bfloat16)
    for g in range(2):
        for z in range(N_ZH):
            for x in range(N_X):
                for c in range(N_C):
                    at = z * 256 + x * 64 + c * 32
                    term_ref[g, x, c, z] = term[at : at + 32, g * 128 : (g + 1) * 128]


def backward(core, own, partner, cots, down_all, slope):
    rows, width = own.shape
    half = N_GRP * 128
    return pl.pallas_call(
        backward_kernel,
        grid_spec=pltpu.PrefetchScalarGridSpec(
            num_scalar_prefetch=1,
            grid=(N_ZH,),
            in_specs=[
                whole(own),
                whole(partner),
                *[whole(c) for c in cots],
                pl.BlockSpec((None, N_X, None, 64, width), lambda q, c: (q, 0, c[0], 0, 0)),
                pl.BlockSpec((2 * rows, 256), lambda q, c: (0, q)),
            ],
            out_specs=pl.BlockSpec((2, N_X, N_C, N_ZH, 32, 128), lambda q, c: (q, 0, 0, 0, 0, 0)),
            scratch_shapes=[pltpu.VMEM((2 * rows, 256), jnp.bfloat16), pltpu.VMEM((2 * rows, width), jnp.bfloat16)],
        ),
        out_shape=jax.ShapeDtypeStruct((N_GRP, N_X, N_C, N_ZH, 32, 128), jnp.bfloat16),
        compiler_params=pltpu.CompilerParams(vmem_limit_bytes=VMEM_BYTES),
        cost_estimate=pl.CostEstimate(
            flops=8 * rows * width * half, bytes_accessed=20 * 1024 * 1024, transcendentals=0
        ),
        name="backward",
    )(core.reshape(1), own, partner, *cots, down_all, slope)


def sum_zh(part, zh):
    total = lax.dynamic_index_in_dim(part, zh, 0, keepdims=False).astype(jnp.float32)
    for step in range(1, N_ZH):
        block = lax.dynamic_index_in_dim(part, (zh + step) % N_ZH, 0, keepdims=False)
        total += shift_zh(block, step).astype(jnp.float32)
    return total.astype(jnp.bfloat16)


def body(reservoir, send_rows, send_count, new_rows, w_up, w_down, ln_gain, grad_new, grad_old):
    slots = send_rows.shape[2]
    fresh_count, width = new_rows.shape
    up_rows, hid = w_up.shape
    group, zh = lax.axis_index(GRP), lax.axis_index("zh")

    down_all = lax.all_gather(w_down, DEV, axis=0, tiled=True).reshape(N_ZH, N_X, N_C, *w_down.shape)
    core = lax.axis_index("c")

    mine = cut_up(w_up, group)
    column = jnp.stack([mine] + [shift_zh(mine, -step) for step in range(1, N_ZH)], axis=1)
    spread_up = jnp.broadcast_to(column[None], (N_GRP * N_X,) + column.shape)
    spread_up = spread_up.reshape(N_GRP * N_X * N_C, N_ZH, up_rows, 128)
    got_up = exchange(spread_up, ("y", "zl", "x", "c")).reshape(N_GRP, N_X, N_C, N_ZH, up_rows, 128)

    grad_new, grad_old, _ = lax.optimization_barrier((grad_new, grad_old, spread_up))
    n_y, n_zl = SIZE["y"], SIZE["zl"]
    y, zl = lax.axis_index("y"), lax.axis_index("zl")
    blocks = grad_old.reshape(n_y, n_zl, slots, width)
    kept = lax.dynamic_index_in_dim(blocks, zl, 1, keepdims=False)
    sent = lax.dynamic_index_in_dim(blocks, 1 - zl, 1, keepdims=False)
    pair = jnp.stack([kept, lax.ppermute(sent, "zl", [(0, 1), (1, 0)])], axis=1)
    order, old_cot = [], []
    for dy in range(n_y):
        block = lax.dynamic_index_in_dim(pair, (y + dy) % n_y, 0, keepdims=False)
        if dy:
            block = lax.ppermute(block, "y", [(i, (i + dy) % n_y) for i in range(n_y)])
        old_cot.append(block.reshape(n_zl * slots, width))
        order += [(y - dy) % n_y * n_zl + zl, (y - dy) % n_y * n_zl + 1 - zl]
    old_cot = jnp.concatenate(old_cot, axis=0)
    order = jnp.stack(order)
    picks, counts = send_rows[0][order], send_count[0][order]
    live = (lax.broadcasted_iota(jnp.int32, (N_GRP, slots), 1) < counts[:, None]).astype(jnp.bfloat16)
    picked = reservoir[picks.reshape(-1)] * live.reshape(-1, 1)

    normed = normalize(jnp.concatenate([new_rows, picked], axis=0), ln_gain)
    partner = swap(normed)
    cots = (grad_new, old_cot, swap(grad_new), swap(old_cot))
    rows = normed.shape[0]

    hidden, slope, term_down = forward(zh, normed, partner, cots, got_up)
    part_down = exchange(term_down.reshape(N_GRP * N_X, N_ZH, 64, 128), ("y", "zl", "x"))
    part_down = jnp.sum(part_down.astype(jnp.float32), axis=0).astype(jnp.bfloat16)
    sum_down = sum_zh(part_down, zh)

    term_up = backward(core, normed, partner, cots, down_all, slope)
    part_up = exchange(term_up.reshape(N_GRP * N_X * N_C, N_ZH, up_rows, 128), ("y", "zl", "x", "c"))
    part_up = part_up.reshape(N_GRP * N_X, N_C, N_ZH, up_rows, 128)
    part_up = jnp.sum(part_up.astype(jnp.float32), axis=0).astype(jnp.bfloat16)
    sum_up = sum_zh(part_up.transpose(1, 0, 2, 3).reshape(N_ZH, N_C * up_rows, 128), zh)

    down_half = lax.dynamic_index_in_dim(down_all, core, 2, keepdims=False).reshape(-1, width)
    other = jnp.dot(hidden[rows : rows + fresh_count], down_half, preferred_element_type=jnp.float32)
    mixed = jnp.dot(hidden[:fresh_count], down_half, preferred_element_type=jnp.float32)
    returned = swap(other.astype(jnp.bfloat16)).astype(jnp.float32)
    block_out = (new_rows.astype(jnp.float32) + (mixed + returned)).astype(jnp.bfloat16)

    both = jnp.stack([sum_down, sum_up])
    both = exchange(jnp.broadcast_to(both[None], (N_GRP,) + both.shape), GRP)
    grad_down, grad_up = finish(both, width, hid)
    return (block_out, grad_up, grad_down)


def solution(mesh):
    fine = Mesh(mesh.devices.reshape(tuple(size for _, size in PHYSICAL)), AXES)
    every = P(AXES, None)
    return jax.shard_map(
        body,
        mesh=fine,
        in_specs=(every, P(AXES, None, None), every, every, P(DEV, None), P(DEV, None), P(), every, every),
        out_specs=(every, P(DEV, None), P(DEV, None)),
        check_vma=False,
    )
```

```python
import jax
import jax.numpy as jnp
from jax import lax
from jax.experimental import pallas as pl
from jax.experimental.pallas import tpu as pltpu
from jax.sharding import Mesh, PartitionSpec as P

PHYSICAL = (("y", 4), ("zl", 2), ("zh", 4), ("x", 4), ("c", 2))
SIZE = dict(PHYSICAL)
AXES = tuple(name for name, _ in PHYSICAL)
GRP = ("y", "zl")
DEV = ("zh", "x", "c")
N_GRP = SIZE["y"] * SIZE["zl"]
N_ZH, N_X, N_C = SIZE["zh"], SIZE["x"], SIZE["c"]
VMEM_BYTES = 48 * 1024 * 1024


def normalize(rows, ln_gain):
    values = rows.astype(jnp.float32)
    center = jnp.mean(values, axis=-1, keepdims=True)
    centred = values - center
    spread = jnp.mean(centred * centred, axis=-1, keepdims=True)
    return (centred * lax.rsqrt(spread + 1e-05) * ln_gain.astype(jnp.float32)).astype(jnp.bfloat16)


def gelu_parts(pre):
    cdf_value = 0.5 * (1.0 + lax.erf(pre * 0.7071067811865476))
    density = jnp.exp(-0.5 * pre * pre) * 0.3989422804014327
    return (pre * cdf_value, cdf_value + pre * density)


def swap(value):
    return lax.ppermute(value, "c", [(0, 1), (1, 0)])


def exchange(value, axes):
    return lax.all_to_all(value, axes, split_axis=0, concat_axis=0, tiled=True)


def shift_zh(value, step):
    return lax.ppermute(value, "zh", [(i, (i + step) % N_ZH) for i in range(N_ZH)])


def lanes_split(left, right):
    low = lax.broadcasted_iota(jnp.int32, left.shape, 1) < 64
    first = jnp.where(low, left, pltpu.roll(right, 64, 1))
    second = jnp.where(low, pltpu.roll(left, 64, 1), right)
    return first, second


def cut_kernel(group_ref, w_ref, out_ref):
    value = w_ref[...].astype(jnp.float32)
    first, second = lanes_split(value[:, :128], value[:, 128:])
    out_ref[0] = first.astype(out_ref.dtype)
    out_ref[1] = second.astype(out_ref.dtype)


def cut_up(w_up, group):
    rows = w_up.shape[0]
    return pl.pallas_call(
        cut_kernel,
        grid_spec=pltpu.PrefetchScalarGridSpec(
            num_scalar_prefetch=1,
            grid=(1,),
            in_specs=[pl.BlockSpec((rows, 256), lambda i, g: (0, g[0]))],
            out_specs=pl.BlockSpec((2, rows, 128), lambda i, g: (0, 0, 0)),
        ),
        out_shape=jax.ShapeDtypeStruct((2, rows, 128), w_up.dtype),
        name="cut_up",
    )(group.reshape(1), w_up)


def final_kernel(both_ref, down_ref, up_ref):
    rows = up_ref.shape[0]
    for g in range(N_GRP):
        down_ref[:, g * 128 : (g + 1) * 128] = both_ref[g, 0].astype(jnp.float32)
        left = both_ref[g, 1, :rows].astype(jnp.float32)
        right = both_ref[g, 1, rows:].astype(jnp.float32)
        first, second = lanes_split(left, right)
        up_ref[:, g * 256 : g * 256 + 128] = first
        up_ref[:, g * 256 + 128 : g * 256 + 256] = second


def finish(both, width, hid):
    rows = both.shape[2]
    return pl.pallas_call(
        final_kernel,
        out_shape=(
            jax.ShapeDtypeStruct((rows, width), jnp.float32),
            jax.ShapeDtypeStruct((rows // N_C, hid), jnp.float32),
        ),
        name="finish",
    )(both)


def join_cot(parts, cot):
    at = 0
    for part in parts:
        cot[at : at + part.shape[0], :] = part[...]
        at += part.shape[0]


def forward_kernel(zh_ref, own_ref, partner_ref, c0, c1, c2, c3, w_ref, hidden_ref, slope_ref, term_ref, w, cot):
    @pl.when(pl.program_id(0) == 0)
    def _():
        join_cot((c0, c1, c2, c3), cot)

    for j in range(N_ZH):
        at = pl.multiple_of(((zh_ref[0] + j) % N_ZH) * 256, 256)
        for g in range(2):
            w[pl.ds(at, 256), g * 128 : (g + 1) * 128] = w_ref[g, :, :, j].reshape(256, 128)
    rows = own_ref.shape[0]
    step = rows // 2
    for which, ref in enumerate((own_ref, partner_ref)):
        for at in range(0, rows, step):
            pre = jnp.dot(ref[at : at + step, :], w[...], preferred_element_type=jnp.float32)
            act, slope = gelu_parts(pre)
            to = which * rows + at
            hidden_ref[to : to + step, :] = act.astype(jnp.bfloat16)
            slope_ref[to : to + step, :] = slope.astype(jnp.bfloat16)
    term = lax.dot_general(hidden_ref[...], cot[...], (((0,), (0,)), ((), ())), preferred_element_type=jnp.float32)
    term = term.astype(jnp.bfloat16)
    for x in range(N_X):
        for g in range(N_GRP):
            term_ref[g, x, 0] = term[x * 64 : (x + 1) * 64, g * 128 : (g + 1) * 128]


def whole(array):
    return pl.BlockSpec(array.shape, lambda *i: (0,) * array.ndim)


def forward(zh, own, partner, cots, got_up):
    rows, width = own.shape
    half = N_GRP * 128
    return pl.pallas_call(
        forward_kernel,
        grid_spec=pltpu.PrefetchScalarGridSpec(
            num_scalar_prefetch=1,
            grid=(N_ZH,),
            in_specs=[
                whole(own),
                whole(partner),
                *[whole(c) for c in cots],
                pl.BlockSpec((2,) + got_up.shape[1:], lambda q, z: (q, 0, 0, 0, 0, 0)),
            ],
            out_specs=[
                pl.BlockSpec((2 * rows, 256), lambda q, z: (0, q)),
                pl.BlockSpec((2 * rows, 256), lambda q, z: (0, q)),
                pl.BlockSpec((N_GRP, N_X, 1, 64, 128), lambda q, z: (0, 0, q, 0, 0)),
            ],
            scratch_shapes=[pltpu.VMEM((width, 256), jnp.bfloat16), pltpu.VMEM((2 * rows, width), jnp.bfloat16)],
        ),
        out_shape=(
            jax.ShapeDtypeStruct((2 * rows, half), jnp.bfloat16),
            jax.ShapeDtypeStruct((2 * rows, half), jnp.bfloat16),
            jax.ShapeDtypeStruct((N_GRP, N_X, N_ZH, 64, 128), jnp.bfloat16),
        ),
        compiler_params=pltpu.CompilerParams(vmem_limit_bytes=VMEM_BYTES),
        cost_estimate=pl.CostEstimate(
            flops=0, bytes_accessed=1024, transcendentals=0
        ),
        name="forward",
    )(zh.reshape(1), own, partner, *cots, got_up)


def backward_kernel(core_ref, own_ref, partner_ref, c0, c1, c2, c3, w_ref, slope_ref, term_ref, pre_grad, cot):
    @pl.when(pl.program_id(0) == 0)
    def _():
        join_cot((c0, c1, c2, c3), cot)

    rows, width = own_ref.shape
    step = rows // 2
    w = w_ref[...].reshape(256, width)
    for at in range(0, 2 * rows, step):
        back = lax.dot_general(
            cot[at : at + step, :], w, (((1,), (1,)), ((), ())), preferred_element_type=jnp.float32
        )
        slope = slope_ref[at : at + step, :].astype(jnp.float32)
        pre_grad[at : at + step, :] = (back * slope).astype(jnp.bfloat16)
    dims = (((0,), (0,)), ((), ()))
    term = lax.dot_general(own_ref[...], pre_grad[:rows, :], dims, preferred_element_type=jnp.float32)
    term += lax.dot_general(partner_ref[...], pre_grad[rows:, :], dims, preferred_element_type=jnp.float32)
    term = term.astype(jnp.bfloat16)
    for g in range(2):
        for z in range(N_ZH):
            for x in range(N_X):
                for c in range(N_C):
                    at = z * 256 + x * 64 + c * 32
                    term_ref[g, x, c, z] = term[at : at + 32, g * 128 : (g + 1) * 128]


def backward(core, own, partner, cots, down_all, slope):
    rows, width = own.shape
    half = N_GRP * 128
    return pl.pallas_call(
        backward_kernel,
        grid_spec=pltpu.PrefetchScalarGridSpec(
            num_scalar_prefetch=1,
            grid=(N_ZH,),
            in_specs=[
                whole(own),
                whole(partner),
                *[whole(c) for c in cots],
                pl.BlockSpec((None, N_X, None, 64, width), lambda q, c: (q, 0, c[0], 0, 0)),
                pl.BlockSpec((2 * rows, 256), lambda q, c: (0, q)),
            ],
            out_specs=pl.BlockSpec((2, N_X, N_C, N_ZH, 32, 128), lambda q, c: (q, 0, 0, 0, 0, 0)),
            scratch_shapes=[pltpu.VMEM((2 * rows, 256), jnp.bfloat16), pltpu.VMEM((2 * rows, width), jnp.bfloat16)],
        ),
        out_shape=jax.ShapeDtypeStruct((N_GRP, N_X, N_C, N_ZH, 32, 128), jnp.bfloat16),
        compiler_params=pltpu.CompilerParams(vmem_limit_bytes=VMEM_BYTES),
        cost_estimate=pl.CostEstimate(
            flops=8 * rows * width * half, bytes_accessed=20 * 1024 * 1024, transcendentals=0
        ),
        name="backward",
    )(core.reshape(1), own, partner, *cots, down_all, slope)


def sum_zh(part, zh):
    total = lax.dynamic_index_in_dim(part, zh, 0, keepdims=False).astype(jnp.float32)
    for step in range(1, N_ZH):
        block = lax.dynamic_index_in_dim(part, (zh + step) % N_ZH, 0, keepdims=False)
        total += shift_zh(block, step).astype(jnp.float32)
    return total.astype(jnp.bfloat16)


def body(reservoir, send_rows, send_count, new_rows, w_up, w_down, ln_gain, grad_new, grad_old):
    slots = send_rows.shape[2]
    fresh_count, width = new_rows.shape
    up_rows, hid = w_up.shape
    group, zh = lax.axis_index(GRP), lax.axis_index("zh")

    down_all = lax.all_gather(w_down, DEV, axis=0, tiled=True).reshape(N_ZH, N_X, N_C, *w_down.shape)
    core = lax.axis_index("c")

    n_y, n_zl = SIZE["y"], SIZE["zl"]
    y, zl = lax.axis_index("y"), lax.axis_index("zl")
    blocks = grad_old.reshape(n_y, n_zl, slots, width)
    kept = lax.dynamic_index_in_dim(blocks, zl, 1, keepdims=False)
    sent = lax.dynamic_index_in_dim(blocks, 1 - zl, 1, keepdims=False)
    pair = jnp.stack([kept, lax.ppermute(sent, "zl", [(0, 1), (1, 0)])], axis=1)
    order, old_cot = [], []
    for dy in range(n_y):
        block = lax.dynamic_index_in_dim(pair, (y + dy) % n_y, 0, keepdims=False)
        if dy:
            block = lax.ppermute(block, "y", [(i, (i + dy) % n_y) for i in range(n_y)])
        old_cot.append(block.reshape(n_zl * slots, width))
        order += [(y - dy) % n_y * n_zl + zl, (y - dy) % n_y * n_zl + 1 - zl]
    order = jnp.stack(order)

    mine = cut_up(w_up, group)
    column = jnp.stack([mine] + [shift_zh(mine, -step) for step in range(1, N_ZH)], axis=1)
    column, *old_cot = lax.optimization_barrier((column, *old_cot))
    old_cot = jnp.concatenate(old_cot, axis=0)
    spread_up = jnp.broadcast_to(column[None], (N_GRP * N_X,) + column.shape)
    spread_up = spread_up.reshape(N_GRP * N_X * N_C, N_ZH, up_rows, 128)
    got_up = exchange(spread_up, ("y", "zl", "x", "c")).reshape(N_GRP, N_X, N_C, N_ZH, up_rows, 128)

    picks, counts = send_rows[0][order], send_count[0][order]
    live = (lax.broadcasted_iota(jnp.int32, (N_GRP, slots), 1) < counts[:, None]).astype(jnp.bfloat16)
    picked = reservoir[picks.reshape(-1)] * live.reshape(-1, 1)

    normed = normalize(jnp.concatenate([new_rows, picked], axis=0), ln_gain)
    partner = swap(normed)
    cots = (grad_new, old_cot, swap(grad_new), swap(old_cot))
    rows = normed.shape[0]

    hidden, slope, term_down = forward(zh, normed, partner, cots, got_up)
    part_down = exchange(term_down.reshape(N_GRP * N_X, N_ZH, 64, 128), ("y", "zl", "x"))
    part_down = jnp.sum(part_down.astype(jnp.float32), axis=0).astype(jnp.bfloat16)
    sum_down = sum_zh(part_down, zh)

    term_up = backward(core, normed, partner, cots, down_all, slope)
    part_up = exchange(term_up.reshape(N_GRP * N_X * N_C, N_ZH, up_rows, 128), ("y", "zl", "x", "c"))
    part_up = part_up.reshape(N_GRP * N_X, N_C, N_ZH, up_rows, 128)
    part_up = jnp.sum(part_up.astype(jnp.float32), axis=0).astype(jnp.bfloat16)
    sum_up = sum_zh(part_up.transpose(1, 0, 2, 3).reshape(N_ZH, N_C * up_rows, 128), zh)

    down_half = lax.dynamic_index_in_dim(down_all, core, 2, keepdims=False).reshape(-1, width)
    other = jnp.dot(hidden[rows : rows + fresh_count], down_half, preferred_element_type=jnp.float32)
    mixed = jnp.dot(hidden[:fresh_count], down_half, preferred_element_type=jnp.float32)
    returned = swap(other.astype(jnp.bfloat16)).astype(jnp.float32)
    block_out = (new_rows.astype(jnp.float32) + (mixed + returned)).astype(jnp.bfloat16)

    both = jnp.stack([sum_down, sum_up])
    both = exchange(jnp.broadcast_to(both[None], (N_GRP,) + both.shape), GRP)
    grad_down, grad_up = finish(both, width, hid)
    return (block_out, grad_up, grad_down)


def solution(mesh):
    fine = Mesh(mesh.devices.reshape(tuple(size for _, size in PHYSICAL)), AXES)
    every = P(AXES, None)
    return jax.shard_map(
        body,
        mesh=fine,
        in_specs=(every, P(AXES, None, None), every, every, P(DEV, None), P(DEV, None), P(), every, every),
        out_specs=(every, P(DEV, None), P(DEV, None)),
        check_vma=False,
    )
```

```python
import jax
import jax.numpy as jnp
from jax import lax
from jax.experimental import pallas as pl
from jax.experimental.pallas import tpu as pltpu
from jax.sharding import Mesh, PartitionSpec as P

PHYSICAL = (("y", 4), ("zl", 2), ("zh", 4), ("x", 4), ("c", 2))
SIZE = dict(PHYSICAL)
AXES = tuple(name for name, _ in PHYSICAL)
GRP = ("y", "zl")
DEV = ("zh", "x", "c")
N_GRP = SIZE["y"] * SIZE["zl"]
N_ZH, N_X, N_C = SIZE["zh"], SIZE["x"], SIZE["c"]
VMEM_BYTES = 48 * 1024 * 1024


def normalize(rows, ln_gain):
    values = rows.astype(jnp.float32)
    center = jnp.mean(values, axis=-1, keepdims=True)
    centred = values - center
    spread = jnp.mean(centred * centred, axis=-1, keepdims=True)
    return (centred * lax.rsqrt(spread + 1e-05) * ln_gain.astype(jnp.float32)).astype(jnp.bfloat16)


def swap(value):
    return lax.ppermute(value, "c", [(0, 1), (1, 0)])


def exchange(value, axes):
    return lax.all_to_all(value, axes, split_axis=0, concat_axis=0, tiled=True)


def shift_zh(value, step):
    return lax.ppermute(value, "zh", [(i, (i + step) % N_ZH) for i in range(N_ZH)])


def lanes_split(left, right):
    low = lax.broadcasted_iota(jnp.int32, left.shape, 1) < 64
    first = jnp.where(low, left, pltpu.roll(right, 64, 1))
    second = jnp.where(low, pltpu.roll(left, 64, 1), right)
    return first, second


def cut_kernel(group_ref, w_ref, out_ref):
    value = w_ref[...].astype(jnp.float32)
    first, second = lanes_split(value[:, :128], value[:, 128:])
    out_ref[0] = first.astype(out_ref.dtype)
    out_ref[1] = second.astype(out_ref.dtype)


def cut_up(w_up, group):
    rows = w_up.shape[0]
    return pl.pallas_call(
        cut_kernel,
        grid_spec=pltpu.PrefetchScalarGridSpec(
            num_scalar_prefetch=1,
            grid=(1,),
            in_specs=[pl.BlockSpec((rows, 256), lambda i, g: (0, g[0]))],
            out_specs=pl.BlockSpec((2, rows, 128), lambda i, g: (0, 0, 0)),
        ),
        out_shape=jax.ShapeDtypeStruct((2, rows, 128), w_up.dtype),
        name="cut_up",
    )(group.reshape(1), w_up)


def final_kernel(both_ref, down_ref, up_ref):
    rows = up_ref.shape[0]
    for g in range(N_GRP):
        down_ref[:, g * 128 : (g + 1) * 128] = both_ref[g, 0].astype(jnp.float32)
        left = both_ref[g, 1, :rows].astype(jnp.float32)
        right = both_ref[g, 1, rows:].astype(jnp.float32)
        first, second = lanes_split(left, right)
        up_ref[:, g * 256 : g * 256 + 128] = first
        up_ref[:, g * 256 + 128 : g * 256 + 256] = second


def finish(both, width, hid):
    rows = both.shape[2]
    return pl.pallas_call(
        final_kernel,
        out_shape=(
            jax.ShapeDtypeStruct((rows, width), jnp.float32),
            jax.ShapeDtypeStruct((rows // N_C, hid), jnp.float32),
        ),
        name="finish",
    )(both)


def join_cot(parts, cot):
    at = 0
    for part in parts:
        cot[at : at + part.shape[0], :] = part[...]
        at += part.shape[0]


def forward_kernel(zh_ref, own_ref, partner_ref, c0, c1, c2, c3, w_ref, hidden_ref, pre_ref, cdf_ref, term_ref, w, cot):
    @pl.when(pl.program_id(0) == 0)
    def _():
        join_cot((c0, c1, c2, c3), cot)

    for j in range(N_ZH):
        at = pl.multiple_of(((zh_ref[0] + j) % N_ZH) * 256, 256)
        for g in range(2):
            w[pl.ds(at, 256), g * 128 : (g + 1) * 128] = w_ref[g, :, :, j].reshape(256, 128)
    rows = own_ref.shape[0]
    step = rows // 2
    for which, ref in enumerate((own_ref, partner_ref)):
        for at in range(0, rows, step):
            pre = jnp.dot(ref[at : at + step, :], w[...], preferred_element_type=jnp.float32)
            cdf_value = 0.5 * (1.0 + lax.erf(pre * 0.7071067811865476))
            to = which * rows + at
            hidden_ref[to : to + step, :] = (pre * cdf_value).astype(jnp.bfloat16)
            pre_ref[to : to + step, :] = pre
            cdf_ref[to : to + step, :] = cdf_value.astype(jnp.bfloat16)
    term = lax.dot_general(hidden_ref[...], cot[...], (((0,), (0,)), ((), ())), preferred_element_type=jnp.float32)
    term = term.astype(jnp.bfloat16)
    for x in range(N_X):
        for g in range(N_GRP):
            term_ref[g, x, 0] = term[x * 64 : (x + 1) * 64, g * 128 : (g + 1) * 128]


def whole(array):
    return pl.BlockSpec(array.shape, lambda *i: (0,) * array.ndim)


def forward(zh, own, partner, cots, got_up):
    rows, width = own.shape
    half = N_GRP * 128
    return pl.pallas_call(
        forward_kernel,
        grid_spec=pltpu.PrefetchScalarGridSpec(
            num_scalar_prefetch=1,
            grid=(N_ZH,),
            in_specs=[
                whole(own),
                whole(partner),
                *[whole(c) for c in cots],
                pl.BlockSpec((2,) + got_up.shape[1:], lambda q, z: (q, 0, 0, 0, 0, 0)),
            ],
            out_specs=[
                pl.BlockSpec((2 * rows, 256), lambda q, z: (0, q)),
                pl.BlockSpec((2 * rows, 256), lambda q, z: (0, q)),
                pl.BlockSpec((2 * rows, 256), lambda q, z: (0, q)),
                pl.BlockSpec((N_GRP, N_X, 1, 64, 128), lambda q, z: (0, 0, q, 0, 0)),
            ],
            scratch_shapes=[pltpu.VMEM((width, 256), jnp.bfloat16), pltpu.VMEM((2 * rows, width), jnp.bfloat16)],
        ),
        out_shape=(
            jax.ShapeDtypeStruct((2 * rows, half), jnp.bfloat16),
            jax.ShapeDtypeStruct((2 * rows, half), jnp.float32),
            jax.ShapeDtypeStruct((2 * rows, half), jnp.bfloat16),
            jax.ShapeDtypeStruct((N_GRP, N_X, N_ZH, 64, 128), jnp.bfloat16),
        ),
        compiler_params=pltpu.CompilerParams(vmem_limit_bytes=VMEM_BYTES),
        cost_estimate=pl.CostEstimate(
            flops=0, bytes_accessed=1024, transcendentals=0
        ),
        name="forward",
    )(zh.reshape(1), own, partner, *cots, got_up)


def backward_kernel(own_ref, partner_ref, c0, c1, c2, c3, w_ref, pre_ref, cdf_ref, term_ref, pre_grad, cot):
    @pl.when(pl.program_id(0) == 0)
    def _():
        join_cot((c0, c1, c2, c3), cot)

    rows, width = own_ref.shape
    step = rows // 2
    w = w_ref[:, :64, :].reshape(256, width)
    for at in range(0, 2 * rows, step):
        back = lax.dot_general(
            cot[at : at + step, :], w, (((1,), (1,)), ((), ())), preferred_element_type=jnp.float32
        )
        pre = pre_ref[at : at + step, :]
        density = jnp.exp(-0.5 * pre * pre) * 0.3989422804014327
        slope = cdf_ref[at : at + step, :].astype(jnp.float32) + pre * density
        pre_grad[at : at + step, :] = (back * slope).astype(jnp.bfloat16)
    dims = (((0,), (0,)), ((), ()))
    term = lax.dot_general(own_ref[...], pre_grad[:rows, :], dims, preferred_element_type=jnp.float32)
    term += lax.dot_general(partner_ref[...], pre_grad[rows:, :], dims, preferred_element_type=jnp.float32)
    term = term.astype(jnp.bfloat16)
    for g in range(2):
        for z in range(N_ZH):
            for x in range(N_X):
                for c in range(N_C):
                    at = z * 256 + x * 64 + c * 32
                    term_ref[g, x, c, z] = term[at : at + 32, g * 128 : (g + 1) * 128]


def backward(own, partner, cots, down_all, pre, cdf_value):
    rows, width = own.shape
    half = N_GRP * 128
    return pl.pallas_call(
        backward_kernel,
        grid_spec=pltpu.PrefetchScalarGridSpec(
            num_scalar_prefetch=0,
            grid=(N_ZH,),
            in_specs=[
                whole(own),
                whole(partner),
                *[whole(c) for c in cots],
                pl.BlockSpec((None, N_X) + down_all.shape[2:], lambda q: (q, 0, 0, 0)),
                pl.BlockSpec((2 * rows, 256), lambda q: (0, q)),
                pl.BlockSpec((2 * rows, 256), lambda q: (0, q)),
            ],
            out_specs=pl.BlockSpec((2, N_X, N_C, N_ZH, 32, 128), lambda q: (q, 0, 0, 0, 0, 0)),
            scratch_shapes=[pltpu.VMEM((2 * rows, 256), jnp.bfloat16), pltpu.VMEM((2 * rows, width), jnp.bfloat16)],
        ),
        out_shape=jax.ShapeDtypeStruct((N_GRP, N_X, N_C, N_ZH, 32, 128), jnp.bfloat16),
        compiler_params=pltpu.CompilerParams(vmem_limit_bytes=VMEM_BYTES),
        cost_estimate=pl.CostEstimate(
            flops=8 * rows * width * half, bytes_accessed=20 * 1024 * 1024, transcendentals=0
        ),
        name="backward",
    )(own, partner, *cots, down_all, pre, cdf_value)


def sum_zh(part, zh):
    total = lax.dynamic_index_in_dim(part, zh, 0, keepdims=False).astype(jnp.float32)
    for step in range(1, N_ZH):
        block = lax.dynamic_index_in_dim(part, (zh + step) % N_ZH, 0, keepdims=False)
        total += shift_zh(block, step).astype(jnp.float32)
    return total.astype(jnp.bfloat16)


def body(reservoir, send_rows, send_count, new_rows, w_up, w_down, ln_gain, grad_new, grad_old):
    slots = send_rows.shape[2]
    fresh_count, width = new_rows.shape
    up_rows, hid = w_up.shape
    group, zh = lax.axis_index(GRP), lax.axis_index("zh")

    down_all = lax.all_gather(jnp.pad(w_down, ((0, 16), (0, 0))), ("zh", "x"), axis=0, tiled=True)
    down_all = down_all.reshape(N_ZH, N_X, -1, width)

    n_y, n_zl = SIZE["y"], SIZE["zl"]
    y, zl = lax.axis_index("y"), lax.axis_index("zl")
    blocks = grad_old.reshape(n_y, n_zl, slots, width)
    kept = lax.dynamic_index_in_dim(blocks, zl, 1, keepdims=False)
    sent = lax.dynamic_index_in_dim(blocks, 1 - zl, 1, keepdims=False)
    pair = jnp.stack([kept, lax.ppermute(sent, "zl", [(0, 1), (1, 0)])], axis=1)
    order, old_cot = [], []
    for dy in range(n_y):
        block = lax.dynamic_index_in_dim(pair, (y + dy) % n_y, 0, keepdims=False)
        if dy:
            block = lax.ppermute(block, "y", [(i, (i + dy) % n_y) for i in range(n_y)])
        old_cot.append(block.reshape(n_zl * slots, width))
        order += [(y - dy) % n_y * n_zl + zl, (y - dy) % n_y * n_zl + 1 - zl]
    order = jnp.stack(order)

    mine = cut_up(w_up, group)
    column = jnp.stack([mine] + [shift_zh(mine, -step) for step in range(1, N_ZH)], axis=1)
    column, *old_cot = lax.optimization_barrier((column, *old_cot))
    old_cot = jnp.concatenate(old_cot, axis=0)
    spread_up = jnp.broadcast_to(column[None], (N_GRP * N_X,) + column.shape)
    spread_up = spread_up.reshape(N_GRP * N_X * N_C, N_ZH, up_rows, 128)
    got_up = exchange(spread_up, ("y", "zl", "x", "c")).reshape(N_GRP, N_X, N_C, N_ZH, up_rows, 128)

    picks, counts = send_rows[0][order], send_count[0][order]
    live = (lax.broadcasted_iota(jnp.int32, (N_GRP, slots), 1) < counts[:, None]).astype(jnp.bfloat16)
    picked = reservoir[picks.reshape(-1)] * live.reshape(-1, 1)

    normed = normalize(jnp.concatenate([new_rows, picked], axis=0), ln_gain)
    partner = swap(normed)
    cots = (grad_new, old_cot, swap(grad_new), swap(old_cot))
    rows = normed.shape[0]

    hidden, pre, cdf_value, term_down = forward(zh, normed, partner, cots, got_up)
    part_down = exchange(term_down.reshape(N_GRP * N_X, N_ZH, 64, 128), ("y", "zl", "x"))
    part_down = jnp.sum(part_down.astype(jnp.float32), axis=0).astype(jnp.bfloat16)
    sum_down = sum_zh(part_down, zh)

    term_up = backward(normed, partner, cots, down_all, pre, cdf_value)
    part_up = exchange(term_up.reshape(N_GRP * N_X * N_C, N_ZH, up_rows, 128), ("y", "zl", "x", "c"))
    part_up = part_up.reshape(N_GRP * N_X, N_C, N_ZH, up_rows, 128)
    part_up = jnp.sum(part_up.astype(jnp.float32), axis=0).astype(jnp.bfloat16)
    sum_up = sum_zh(part_up.transpose(1, 0, 2, 3).reshape(N_ZH, N_C * up_rows, 128), zh)

    down_half = down_all[:, :, :64].reshape(-1, width)
    other = jnp.dot(hidden[rows : rows + fresh_count], down_half, preferred_element_type=jnp.float32)
    mixed = jnp.dot(hidden[:fresh_count], down_half, preferred_element_type=jnp.float32)
    returned = swap(other.astype(jnp.bfloat16)).astype(jnp.float32)
    block_out = (new_rows.astype(jnp.float32) + (mixed + returned)).astype(jnp.bfloat16)

    both = jnp.stack([sum_down, sum_up])
    both = exchange(jnp.broadcast_to(both[None], (N_GRP,) + both.shape), GRP)
    grad_down, grad_up = finish(both, width, hid)
    return (block_out, grad_up, grad_down)


def solution(mesh):
    fine = Mesh(mesh.devices.reshape(tuple(size for _, size in PHYSICAL)), AXES)
    every = P(AXES, None)
    return jax.shard_map(
        body,
        mesh=fine,
        in_specs=(every, P(AXES, None, None), every, every, P(DEV, None), P(DEV, None), P(), every, every),
        out_specs=(every, P(DEV, None), P(DEV, None)),
        check_vma=False,
    )
```

```python
import jax
import jax.numpy as jnp
from jax import lax
from jax.experimental import pallas as pl
from jax.experimental.pallas import tpu as pltpu
from jax.sharding import Mesh, PartitionSpec as P

PHYSICAL = (("y", 4), ("zl", 2), ("zh", 4), ("x", 4), ("c", 2))
SIZE = dict(PHYSICAL)
AXES = tuple(name for name, _ in PHYSICAL)
GRP = ("y", "zl")
DEV = ("zh", "x", "c")
N_GRP = SIZE["y"] * SIZE["zl"]
N_ZH, N_X, N_C = SIZE["zh"], SIZE["x"], SIZE["c"]
VMEM_BYTES = 48 * 1024 * 1024


def normalize(rows, ln_gain):
    values = rows.astype(jnp.float32)
    center = jnp.mean(values, axis=-1, keepdims=True)
    centred = values - center
    spread = jnp.mean(centred * centred, axis=-1, keepdims=True)
    return (centred * lax.rsqrt(spread + 1e-05) * ln_gain.astype(jnp.float32)).astype(jnp.bfloat16)


def swap(value):
    return lax.ppermute(value, "c", [(0, 1), (1, 0)])


def exchange(value, axes):
    return lax.all_to_all(value, axes, split_axis=0, concat_axis=0, tiled=True)


def shift(value, axis, step):
    n = SIZE[axis]
    return lax.ppermute(value, axis, [(i, (i + step) % n) for i in range(n)])


def along(value, axis):
    return [value] + [shift(value, axis, -step) for step in range(1, SIZE[axis])]


def whole(array):
    return pl.BlockSpec(array.shape, lambda *i: (0,) * array.ndim)


def lanes_split(left, right):
    low = lax.broadcasted_iota(jnp.int32, left.shape, 1) < 64
    first = jnp.where(low, left, pltpu.roll(right, 64, 1))
    second = jnp.where(low, pltpu.roll(left, 64, 1), right)
    return first, second


def cut_kernel(at_ref, up_ref, down_ref, out_ref):
    rows = up_ref.shape[0]
    value = up_ref[...].astype(jnp.float32)
    first, second = lanes_split(value[:, :128], value[:, 128:])
    out_ref[:rows, :128] = first.astype(out_ref.dtype)
    out_ref[rows:, :128] = second.astype(out_ref.dtype)
    out_ref[:, 128:] = down_ref[...]


def cut(w_up, w_down, group, y):
    up_rows, down_rows = w_up.shape[0], w_down.shape[0]
    return pl.pallas_call(
        cut_kernel,
        grid_spec=pltpu.PrefetchScalarGridSpec(
            num_scalar_prefetch=1,
            grid=(1,),
            in_specs=[
                pl.BlockSpec((up_rows, 256), lambda i, at: (0, at[0])),
                pl.BlockSpec((down_rows, 256), lambda i, at: (0, at[1])),
            ],
            out_specs=pl.BlockSpec((down_rows, 384), lambda i, at: (0, 0)),
        ),
        out_shape=jax.ShapeDtypeStruct((down_rows, 384), w_up.dtype),
        name="cut",
    )(jnp.stack([group, y]), w_up, w_down)


def spread_kernel(p0, p1, p2, p3, spread_ref, down_ref):
    rows = spread_ref.shape[3]
    for j, part in enumerate((p0, p1, p2, p3)):
        down_ref[j] = part[:, 128:]
        for c in range(N_C):
            value = part[c * rows : (c + 1) * rows, :128]
            for n in range(spread_ref.shape[0]):
                spread_ref[n, c, j] = value


def spread(parts):
    down_rows = parts[0].shape[0]
    rows = down_rows // N_C
    return pl.pallas_call(
        spread_kernel,
        grid=(N_GRP,),
        in_specs=[whole(part) for part in parts],
        out_specs=[
            pl.BlockSpec((N_X, N_C, N_ZH, rows, 128), lambda i: (i, 0, 0, 0, 0)),
            pl.BlockSpec((N_ZH, down_rows, 256), lambda i: (0, 0, 0)),
        ],
        out_shape=(
            jax.ShapeDtypeStruct((N_GRP * N_X, N_C, N_ZH, rows, 128), parts[0].dtype),
            jax.ShapeDtypeStruct((N_ZH, down_rows, 256), parts[0].dtype),
        ),
        name="spread",
    )(*parts)


def final_kernel(both_ref, down_ref, up_ref):
    rows = up_ref.shape[0]
    for g in range(N_GRP):
        down_ref[:, g * 128 : (g + 1) * 128] = both_ref[g, 0].astype(jnp.float32)
        left = both_ref[g, 1, :rows].astype(jnp.float32)
        right = both_ref[g, 1, rows:].astype(jnp.float32)
        first, second = lanes_split(left, right)
        up_ref[:, g * 256 : g * 256 + 128] = first
        up_ref[:, g * 256 + 128 : g * 256 + 256] = second


def finish(both, width, hid):
    rows = both.shape[2]
    return pl.pallas_call(
        final_kernel,
        out_shape=(
            jax.ShapeDtypeStruct((rows, width), jnp.float32),
            jax.ShapeDtypeStruct((rows // N_C, hid), jnp.float32),
        ),
        name="finish",
    )(both)


def join_cot(parts, cot):
    at = 0
    for part in parts:
        cot[at : at + part.shape[0], :] = part[...]
        at += part.shape[0]


def forward_kernel(zh_ref, own_ref, partner_ref, c0, c1, c2, c3, w_ref, hidden_ref, pre_ref, cdf_ref, term_ref, w, cot):
    @pl.when(pl.program_id(0) == 0)
    def _():
        join_cot((c0, c1, c2, c3), cot)

    for j in range(N_ZH):
        at = pl.multiple_of(((zh_ref[0] + j) % N_ZH) * 256, 256)
        for g in range(2):
            w[pl.ds(at, 256), g * 128 : (g + 1) * 128] = w_ref[g, :, :, j].reshape(256, 128)
    rows = own_ref.shape[0]
    step = rows // 2
    for which, ref in enumerate((own_ref, partner_ref)):
        for at in range(0, rows, step):
            pre = jnp.dot(ref[at : at + step, :], w[...], preferred_element_type=jnp.float32)
            cdf_value = 0.5 * (1.0 + lax.erf(pre * 0.7071067811865476))
            to = which * rows + at
            hidden_ref[to : to + step, :] = (pre * cdf_value).astype(jnp.bfloat16)
            pre_ref[to : to + step, :] = pre
            cdf_ref[to : to + step, :] = cdf_value.astype(jnp.bfloat16)
    term = lax.dot_general(hidden_ref[...], cot[...], (((0,), (0,)), ((), ())), preferred_element_type=jnp.float32)
    term = term.astype(jnp.bfloat16)
    for x in range(N_X):
        for g in range(N_GRP):
            term_ref[g, x, 0] = term[x * 64 : (x + 1) * 64, g * 128 : (g + 1) * 128]


def forward(zh, own, partner, cots, got_up):
    rows, width = own.shape
    half = N_GRP * 128
    return pl.pallas_call(
        forward_kernel,
        grid_spec=pltpu.PrefetchScalarGridSpec(
            num_scalar_prefetch=1,
            grid=(N_ZH,),
            in_specs=[
                whole(own),
                whole(partner),
                *[whole(c) for c in cots],
                pl.BlockSpec((2,) + got_up.shape[1:], lambda q, z: (q, 0, 0, 0, 0, 0)),
            ],
            out_specs=[
                pl.BlockSpec((2 * rows, 256), lambda q, z: (0, q)),
                pl.BlockSpec((2 * rows, 256), lambda q, z: (0, q)),
                pl.BlockSpec((2 * rows, 256), lambda q, z: (0, q)),
                pl.BlockSpec((N_GRP, N_X, 1, 64, 128), lambda q, z: (0, 0, q, 0, 0)),
            ],
            scratch_shapes=[pltpu.VMEM((width, 256), jnp.bfloat16), pltpu.VMEM((2 * rows, width), jnp.bfloat16)],
        ),
        out_shape=(
            jax.ShapeDtypeStruct((2 * rows, half), jnp.bfloat16),
            jax.ShapeDtypeStruct((2 * rows, half), jnp.float32),
            jax.ShapeDtypeStruct((2 * rows, half), jnp.bfloat16),
            jax.ShapeDtypeStruct((N_GRP, N_X, N_ZH, 64, 128), jnp.bfloat16),
        ),
        compiler_params=pltpu.CompilerParams(vmem_limit_bytes=VMEM_BYTES),
        cost_estimate=pl.CostEstimate(
            flops=0, bytes_accessed=1024, transcendentals=0
        ),
        name="forward",
    )(zh.reshape(1), own, partner, *cots, got_up)


def backward_kernel(at_ref, own_ref, partner_ref, c0, c1, c2, c3, w0, w1, w2, w3, pre_ref, cdf_ref, term_ref, w, pre_grad, cot):
    @pl.when(pl.program_id(0) == 0)
    def _():
        join_cot((c0, c1, c2, c3), cot)

    rows, width = own_ref.shape
    step = rows // 2
    for j, ref in enumerate((w0, w1, w2, w3)):
        column = pl.multiple_of((at_ref[1] + j) % SIZE["y"] * 256, 256)
        for i in range(N_X):
            row = pl.multiple_of((at_ref[2] + i) % N_X * 64, 64)
            w[pl.ds(row, 64), pl.ds(column, 256)] = ref[i, 0]
    for at in range(0, 2 * rows, step):
        back = lax.dot_general(
            cot[at : at + step, :], w[...], (((1,), (1,)), ((), ())), preferred_element_type=jnp.float32
        )
        pre = pre_ref[at : at + step, :]
        density = jnp.exp(-0.5 * pre * pre) * 0.3989422804014327
        slope = cdf_ref[at : at + step, :].astype(jnp.float32) + pre * density
        pre_grad[at : at + step, :] = (back * slope).astype(jnp.bfloat16)
    dims = (((0,), (0,)), ((), ()))
    term = lax.dot_general(own_ref[...], pre_grad[:rows, :], dims, preferred_element_type=jnp.float32)
    term += lax.dot_general(partner_ref[...], pre_grad[rows:, :], dims, preferred_element_type=jnp.float32)
    term = term.astype(jnp.bfloat16)
    for g in range(2):
        for z in range(N_ZH):
            for x in range(N_X):
                for c in range(N_C):
                    at = z * 256 + x * 64 + c * 32
                    term_ref[g, x, c, z] = term[at : at + 32, g * 128 : (g + 1) * 128]


def backward(at, own, partner, cots, downs, pre, cdf_value):
    rows, width = own.shape
    half = N_GRP * 128
    return pl.pallas_call(
        backward_kernel,
        grid_spec=pltpu.PrefetchScalarGridSpec(
            num_scalar_prefetch=1,
            grid=(N_ZH,),
            in_specs=[
                whole(own),
                whole(partner),
                *[whole(c) for c in cots],
                *[pl.BlockSpec((N_X, 1, 64, 256), lambda q, at: (0, (q - at[0] + N_ZH) % N_ZH, 0, 0)) for _ in downs],
                pl.BlockSpec((2 * rows, 256), lambda q, at: (0, q)),
                pl.BlockSpec((2 * rows, 256), lambda q, at: (0, q)),
            ],
            out_specs=[
                pl.BlockSpec((2, N_X, N_C, N_ZH, 32, 128), lambda q, at: (q, 0, 0, 0, 0, 0)),
                pl.BlockSpec((256, width), lambda q, at: (q, 0)),
            ],
            scratch_shapes=[pltpu.VMEM((2 * rows, 256), jnp.bfloat16), pltpu.VMEM((2 * rows, width), jnp.bfloat16)],
        ),
        out_shape=(
            jax.ShapeDtypeStruct((N_GRP, N_X, N_C, N_ZH, 32, 128), jnp.bfloat16),
            jax.ShapeDtypeStruct((half, width), jnp.bfloat16),
        ),
        compiler_params=pltpu.CompilerParams(vmem_limit_bytes=VMEM_BYTES),
        cost_estimate=pl.CostEstimate(
            flops=8 * rows * width * half, bytes_accessed=20 * 1024 * 1024, transcendentals=0
        ),
        name="backward",
    )(at, own, partner, *cots, *downs, pre, cdf_value)


def sum_zh(part, zh):
    total = lax.dynamic_index_in_dim(part, zh, 0, keepdims=False).astype(jnp.float32)
    for step in range(1, N_ZH):
        block = lax.dynamic_index_in_dim(part, (zh + step) % N_ZH, 0, keepdims=False)
        total += shift(block, "zh", step).astype(jnp.float32)
    return total.astype(jnp.bfloat16)


def body(reservoir, send_rows, send_count, new_rows, w_up, w_down, ln_gain, grad_new, grad_old):
    slots = send_rows.shape[2]
    fresh_count, width = new_rows.shape
    up_rows, hid = w_up.shape
    group, zh = lax.axis_index(GRP), lax.axis_index("zh")

    n_y, n_zl = SIZE["y"], SIZE["zl"]
    y, zl = lax.axis_index("y"), lax.axis_index("zl")
    blocks = grad_old.reshape(n_y, n_zl, slots, width)
    kept = lax.dynamic_index_in_dim(blocks, zl, 1, keepdims=False)
    sent = lax.dynamic_index_in_dim(blocks, 1 - zl, 1, keepdims=False)
    pair = jnp.stack([kept, lax.ppermute(sent, "zl", [(0, 1), (1, 0)])], axis=1)
    order, old_cot = [], []
    for dy in range(n_y):
        block = lax.dynamic_index_in_dim(pair, (y + dy) % n_y, 0, keepdims=False)
        if dy:
            block = lax.ppermute(block, "y", [(i, (i + dy) % n_y) for i in range(n_y)])
        old_cot.append(block.reshape(n_zl * slots, width))
        order += [(y - dy) % n_y * n_zl + zl, (y - dy) % n_y * n_zl + 1 - zl]
    order = jnp.stack(order)

    parts = along(cut(w_up, w_down, group, y), "zh")
    both = lax.optimization_barrier((*parts, *old_cot))
    parts, old_cot = both[: len(parts)], jnp.concatenate(both[len(parts) :], axis=0)
    spread_up, down_zh = spread(parts)
    spread_up = spread_up.reshape(N_GRP * N_X * N_C, N_ZH, up_rows, 128)
    got_up = exchange(spread_up, ("y", "zl", "x", "c")).reshape(N_GRP, N_X, N_C, N_ZH, up_rows, 128)
    downs = along(jnp.stack(along(down_zh, "x")), "y")

    picks, counts = send_rows[0][order], send_count[0][order]
    live = (lax.broadcasted_iota(jnp.int32, (N_GRP, slots), 1) < counts[:, None]).astype(jnp.bfloat16)
    picked = reservoir[picks.reshape(-1)] * live.reshape(-1, 1)

    normed = normalize(jnp.concatenate([new_rows, picked], axis=0), ln_gain)
    partner = swap(normed)
    cots = (grad_new, old_cot, swap(grad_new), swap(old_cot))
    rows = normed.shape[0]

    hidden, pre, cdf_value, term_down = forward(zh, normed, partner, cots, got_up)
    term_down, *downs = lax.optimization_barrier((term_down, *downs))
    part_down = exchange(term_down.reshape(N_GRP * N_X, N_ZH, 64, 128), ("y", "zl", "x"))
    part_down = jnp.sum(part_down.astype(jnp.float32), axis=0).astype(jnp.bfloat16)
    sum_down = sum_zh(part_down, zh)

    at = jnp.stack([zh, y, lax.axis_index("x")])
    term_up, down_half = backward(at, normed, partner, cots, downs, pre, cdf_value)
    part_up = exchange(term_up.reshape(N_GRP * N_X * N_C, N_ZH, up_rows, 128), ("y", "zl", "x", "c"))
    part_up = part_up.reshape(N_GRP * N_X, N_C, N_ZH, up_rows, 128)
    part_up = jnp.sum(part_up.astype(jnp.float32), axis=0).astype(jnp.bfloat16)
    sum_up = sum_zh(part_up.transpose(1, 0, 2, 3).reshape(N_ZH, N_C * up_rows, 128), zh)

    other = jnp.dot(hidden[rows : rows + fresh_count], down_half, preferred_element_type=jnp.float32)
    mixed = jnp.dot(hidden[:fresh_count], down_half, preferred_element_type=jnp.float32)
    returned = swap(other.astype(jnp.bfloat16)).astype(jnp.float32)
    block_out = (new_rows.astype(jnp.float32) + (mixed + returned)).astype(jnp.bfloat16)

    both = jnp.stack([sum_down, sum_up])
    both = exchange(jnp.broadcast_to(both[None], (N_GRP,) + both.shape), GRP)
    grad_down, grad_up = finish(both, width, hid)
    return (block_out, grad_up, grad_down)


def solution(mesh):
    fine = Mesh(mesh.devices.reshape(tuple(size for _, size in PHYSICAL)), AXES)
    every = P(AXES, None)
    return jax.shard_map(
        body,
        mesh=fine,
        in_specs=(every, P(AXES, None, None), every, every, P(DEV, None), P(DEV, None), P(), every, every),
        out_specs=(every, P(DEV, None), P(DEV, None)),
        check_vma=False,
    )
```

```python
import jax
import jax.numpy as jnp
from jax import lax
from jax.experimental import pallas as pl
from jax.experimental.pallas import tpu as pltpu
from jax.sharding import Mesh, PartitionSpec as P

PHYSICAL = (("y", 4), ("zl", 2), ("zh", 4), ("x", 4), ("c", 2))
SIZE = dict(PHYSICAL)
AXES = tuple(name for name, _ in PHYSICAL)
GRP = ("y", "zl")
DEV = ("zh", "x", "c")
N_GRP = SIZE["y"] * SIZE["zl"]
N_ZH, N_X, N_C = SIZE["zh"], SIZE["x"], SIZE["c"]
VMEM_BYTES = 48 * 1024 * 1024


def normalize(rows, ln_gain):
    values = rows.astype(jnp.float32)
    center = jnp.mean(values, axis=-1, keepdims=True)
    centred = values - center
    spread = jnp.mean(centred * centred, axis=-1, keepdims=True)
    return (centred * lax.rsqrt(spread + 1e-05) * ln_gain.astype(jnp.float32)).astype(jnp.bfloat16)


def swap(value):
    return lax.ppermute(value, "c", [(0, 1), (1, 0)])


def exchange(value, axes):
    return lax.all_to_all(value, axes, split_axis=0, concat_axis=0, tiled=True)


def shift(value, axis, step):
    n = SIZE[axis]
    return lax.ppermute(value, axis, [(i, (i + step) % n) for i in range(n)])


def along(value, axis):
    return [value] + [shift(value, axis, -step) for step in range(1, SIZE[axis])]


def whole(array):
    return pl.BlockSpec(array.shape, lambda *i: (0,) * array.ndim)


def lanes_split(left, right):
    low = lax.broadcasted_iota(jnp.int32, left.shape, 1) < 64
    first = jnp.where(low, left, pltpu.roll(right, 64, 1))
    second = jnp.where(low, pltpu.roll(left, 64, 1), right)
    return first, second


def cut_kernel(at_ref, up_ref, down_ref, out_ref):
    rows = up_ref.shape[0]
    value = up_ref[...].astype(jnp.float32)
    first, second = lanes_split(value[:, :128], value[:, 128:])
    out_ref[:rows, :128] = first.astype(out_ref.dtype)
    out_ref[rows:, :128] = second.astype(out_ref.dtype)
    out_ref[:, 128:] = down_ref[...]


def cut(w_up, w_down, group, y):
    up_rows, down_rows = w_up.shape[0], w_down.shape[0]
    return pl.pallas_call(
        cut_kernel,
        grid_spec=pltpu.PrefetchScalarGridSpec(
            num_scalar_prefetch=1,
            grid=(1,),
            in_specs=[
                pl.BlockSpec((up_rows, 256), lambda i, at: (0, at[0])),
                pl.BlockSpec((down_rows, 256), lambda i, at: (0, at[1])),
            ],
            out_specs=pl.BlockSpec((down_rows, 384), lambda i, at: (0, 0)),
        ),
        out_shape=jax.ShapeDtypeStruct((down_rows, 384), w_up.dtype),
        name="cut",
    )(jnp.stack([group, y]), w_up, w_down)


def spread_kernel(p0, p1, p2, p3, spread_ref, down_ref):
    rows = spread_ref.shape[3]
    for j, part in enumerate((p0, p1, p2, p3)):
        down_ref[j] = part[:, 128:]
        for c in range(N_C):
            value = part[c * rows : (c + 1) * rows, :128]
            for n in range(spread_ref.shape[0]):
                spread_ref[n, c, j] = value


def spread(parts):
    down_rows = parts[0].shape[0]
    rows = down_rows // N_C
    return pl.pallas_call(
        spread_kernel,
        grid=(2,),
        in_specs=[whole(part) for part in parts],
        out_specs=[
            pl.BlockSpec((N_GRP * N_X // 2, N_C, N_ZH, rows, 128), lambda i: (i, 0, 0, 0, 0)),
            pl.BlockSpec((N_ZH, down_rows, 256), lambda i: (0, 0, 0)),
        ],
        out_shape=(
            jax.ShapeDtypeStruct((N_GRP * N_X, N_C, N_ZH, rows, 128), parts[0].dtype),
            jax.ShapeDtypeStruct((N_ZH, down_rows, 256), parts[0].dtype),
        ),
        name="spread",
    )(*parts)


def final_kernel(both_ref, down_ref, up_ref):
    rows = up_ref.shape[0]
    for g in range(N_GRP):
        down_ref[:, g * 128 : (g + 1) * 128] = both_ref[g, 0].astype(jnp.float32)
        left = both_ref[g, 1, :rows].astype(jnp.float32)
        right = both_ref[g, 1, rows:].astype(jnp.float32)
        first, second = lanes_split(left, right)
        up_ref[:, g * 256 : g * 256 + 128] = first
        up_ref[:, g * 256 + 128 : g * 256 + 256] = second


def finish(both, width, hid):
    rows = both.shape[2]
    return pl.pallas_call(
        final_kernel,
        out_shape=(
            jax.ShapeDtypeStruct((rows, width), jnp.float32),
            jax.ShapeDtypeStruct((rows // N_C, hid), jnp.float32),
        ),
        name="finish",
    )(both)


def join_cot(parts, cot):
    at = 0
    for part in parts:
        cot[at : at + part.shape[0], :] = part[...]
        at += part.shape[0]


def forward_kernel(zh_ref, own_ref, partner_ref, c0, c1, w_ref, hidden_ref, pre_ref, cdf_ref, term_ref, w, cot):
    @pl.when(pl.program_id(0) == 0)
    def _():
        join_cot((c0, c1), cot)

    for j in range(N_ZH):
        at = pl.multiple_of(((zh_ref[0] + j) % N_ZH) * 256, 256)
        for g in range(2):
            w[pl.ds(at, 256), g * 128 : (g + 1) * 128] = w_ref[g, :, :, j].reshape(256, 128)
    rows = own_ref.shape[0]
    step = rows // 2
    for which, ref in enumerate((own_ref, partner_ref)):
        for at in range(0, rows, step):
            pre = jnp.dot(ref[at : at + step, :], w[...], preferred_element_type=jnp.float32)
            cdf_value = 0.5 * (1.0 + lax.erf(pre * 0.7071067811865476))
            to = which * rows + at
            hidden_ref[to : to + step, :] = (pre * cdf_value).astype(jnp.bfloat16)
            pre_ref[to : to + step, :] = pre
            cdf_ref[to : to + step, :] = cdf_value.astype(jnp.bfloat16)
    term = lax.dot_general(hidden_ref[...], cot[...], (((0,), (0,)), ((), ())), preferred_element_type=jnp.float32)
    term = term.astype(jnp.bfloat16)
    for x in range(N_X):
        for g in range(N_GRP):
            term_ref[g, x, 0] = term[x * 64 : (x + 1) * 64, g * 128 : (g + 1) * 128]


def forward(zh, own, partner, cots, got_up):
    rows, width = own.shape
    half = N_GRP * 128
    return pl.pallas_call(
        forward_kernel,
        grid_spec=pltpu.PrefetchScalarGridSpec(
            num_scalar_prefetch=1,
            grid=(N_ZH,),
            in_specs=[
                whole(own),
                whole(partner),
                *[whole(c) for c in cots],
                pl.BlockSpec((2,) + got_up.shape[1:], lambda q, z: (q, 0, 0, 0, 0, 0)),
            ],
            out_specs=[
                pl.BlockSpec((2 * rows, 256), lambda q, z: (0, q)),
                pl.BlockSpec((2 * rows, 256), lambda q, z: (0, q)),
                pl.BlockSpec((2 * rows, 256), lambda q, z: (0, q)),
                pl.BlockSpec((N_GRP, N_X, 1, 64, 128), lambda q, z: (0, 0, q, 0, 0)),
            ],
            scratch_shapes=[pltpu.VMEM((width, 256), jnp.bfloat16), pltpu.VMEM((2 * rows, width), jnp.bfloat16)],
        ),
        out_shape=(
            jax.ShapeDtypeStruct((2 * rows, half), jnp.bfloat16),
            jax.ShapeDtypeStruct((2 * rows, half), jnp.float32),
            jax.ShapeDtypeStruct((2 * rows, half), jnp.bfloat16),
            jax.ShapeDtypeStruct((N_GRP, N_X, N_ZH, 64, 128), jnp.bfloat16),
        ),
        compiler_params=pltpu.CompilerParams(vmem_limit_bytes=VMEM_BYTES),
        cost_estimate=pl.CostEstimate(
            flops=0, bytes_accessed=1024, transcendentals=0
        ),
        name="forward",
    )(zh.reshape(1), own, partner, *cots, got_up)


def backward_kernel(at_ref, own_ref, partner_ref, c0, c1, w0, w1, w2, w3, pre_ref, cdf_ref, term_ref, w, pre_grad, cot):
    @pl.when(pl.program_id(0) == 0)
    def _():
        join_cot((c0, c1), cot)

    rows, width = own_ref.shape
    step = rows // 2
    for j, ref in enumerate((w0, w1, w2, w3)):
        column = pl.multiple_of((at_ref[1] + j) % SIZE["y"] * 256, 256)
        for i in range(N_X):
            row = pl.multiple_of((at_ref[2] + i) % N_X * 64, 64)
            w[pl.ds(row, 64), pl.ds(column, 256)] = ref[i, 0]
    for at in range(0, 2 * rows, step):
        back = lax.dot_general(
            cot[at : at + step, :], w[...], (((1,), (1,)), ((), ())), preferred_element_type=jnp.float32
        )
        pre = pre_ref[at : at + step, :]
        density = jnp.exp(-0.5 * pre * pre) * 0.3989422804014327
        slope = cdf_ref[at : at + step, :].astype(jnp.float32) + pre * density
        pre_grad[at : at + step, :] = (back * slope).astype(jnp.bfloat16)
    dims = (((0,), (0,)), ((), ()))
    term = lax.dot_general(own_ref[...], pre_grad[:rows, :], dims, preferred_element_type=jnp.float32)
    term += lax.dot_general(partner_ref[...], pre_grad[rows:, :], dims, preferred_element_type=jnp.float32)
    term = term.astype(jnp.bfloat16)
    for g in range(2):
        for z in range(N_ZH):
            for x in range(N_X):
                for c in range(N_C):
                    at = z * 256 + x * 64 + c * 32
                    term_ref[g, x, c, z] = term[at : at + 32, g * 128 : (g + 1) * 128]


def backward(at, own, partner, cots, downs, pre, cdf_value):
    rows, width = own.shape
    half = N_GRP * 128
    return pl.pallas_call(
        backward_kernel,
        grid_spec=pltpu.PrefetchScalarGridSpec(
            num_scalar_prefetch=1,
            grid=(N_ZH,),
            in_specs=[
                whole(own),
                whole(partner),
                *[whole(c) for c in cots],
                *[pl.BlockSpec((N_X, 1, 64, 256), lambda q, at: (0, (q - at[0] + N_ZH) % N_ZH, 0, 0)) for _ in downs],
                pl.BlockSpec((2 * rows, 256), lambda q, at: (0, q)),
                pl.BlockSpec((2 * rows, 256), lambda q, at: (0, q)),
            ],
            out_specs=[
                pl.BlockSpec((2, N_X, N_C, N_ZH, 32, 128), lambda q, at: (q, 0, 0, 0, 0, 0)),
                pl.BlockSpec((256, width), lambda q, at: (q, 0)),
            ],
            scratch_shapes=[pltpu.VMEM((2 * rows, 256), jnp.bfloat16), pltpu.VMEM((2 * rows, width), jnp.bfloat16)],
        ),
        out_shape=(
            jax.ShapeDtypeStruct((N_GRP, N_X, N_C, N_ZH, 32, 128), jnp.bfloat16),
            jax.ShapeDtypeStruct((half, width), jnp.bfloat16),
        ),
        compiler_params=pltpu.CompilerParams(vmem_limit_bytes=VMEM_BYTES),
        cost_estimate=pl.CostEstimate(
            flops=400 * rows * width * half, bytes_accessed=20 * 1024 * 1024, transcendentals=0
        ),
        name="backward",
    )(at, own, partner, *cots, *downs, pre, cdf_value)


def sum_zh(part, zh):
    total = lax.dynamic_index_in_dim(part, zh, 0, keepdims=False).astype(jnp.float32)
    for step in range(1, N_ZH):
        block = lax.dynamic_index_in_dim(part, (zh + step) % N_ZH, 0, keepdims=False)
        total += shift(block, "zh", step).astype(jnp.float32)
    return total.astype(jnp.bfloat16)


def body(reservoir, send_rows, send_count, new_rows, w_up, w_down, ln_gain, grad_new, grad_old):
    slots = send_rows.shape[2]
    fresh_count, width = new_rows.shape
    up_rows, hid = w_up.shape
    group, zh = lax.axis_index(GRP), lax.axis_index("zh")

    n_y, n_zl = SIZE["y"], SIZE["zl"]
    y, zl = lax.axis_index("y"), lax.axis_index("zl")
    blocks = grad_old.reshape(n_y, n_zl, slots, width)
    kept = lax.dynamic_index_in_dim(blocks, zl, 1, keepdims=False)
    sent = lax.dynamic_index_in_dim(blocks, 1 - zl, 1, keepdims=False)
    pair = jnp.stack([kept, lax.ppermute(sent, "zl", [(0, 1), (1, 0)])], axis=1)
    parts = along(cut(w_up, w_down, group, y), "zh")
    pair, *parts = lax.optimization_barrier((pair, *parts))
    order, old_cot = [], []
    for dy in range(n_y):
        block = lax.dynamic_index_in_dim(pair, (y + dy) % n_y, 0, keepdims=False)
        if dy:
            block = lax.ppermute(block, "y", [(i, (i + dy) % n_y) for i in range(n_y)])
        old_cot.append(block.reshape(n_zl * slots, width))
        order += [(y - dy) % n_y * n_zl + zl, (y - dy) % n_y * n_zl + 1 - zl]
    order = jnp.stack(order)

    spread_up, down_zh = spread(parts)
    spread_up, *old_cot = lax.optimization_barrier((spread_up, *old_cot))
    cot = jnp.concatenate([grad_new, *old_cot], axis=0)
    spread_up = spread_up.reshape(N_GRP * N_X * N_C, N_ZH, up_rows, 128)
    got_up = exchange(spread_up, ("y", "zl", "x", "c")).reshape(N_GRP, N_X, N_C, N_ZH, up_rows, 128)
    downs = along(jnp.stack(along(down_zh, "x")), "y")

    picks, counts = send_rows[0][order], send_count[0][order]
    live = (lax.broadcasted_iota(jnp.int32, (N_GRP, slots), 1) < counts[:, None]).astype(jnp.bfloat16)
    picked = reservoir[picks.reshape(-1)] * live.reshape(-1, 1)

    normed = normalize(jnp.concatenate([new_rows, picked], axis=0), ln_gain)
    partner = swap(normed)
    cots = (cot, swap(cot))
    rows = normed.shape[0]

    hidden, pre, cdf_value, term_down = forward(zh, normed, partner, cots, got_up)
    part_down = exchange(term_down.reshape(N_GRP * N_X, N_ZH, 64, 128), ("y", "zl", "x"))
    part_down = jnp.sum(part_down.astype(jnp.float32), axis=0).astype(jnp.bfloat16)
    sum_down = sum_zh(part_down, zh)

    at = jnp.stack([zh, y, lax.axis_index("x")])
    term_up, down_half = backward(at, normed, partner, cots, downs, pre, cdf_value)
    part_up = exchange(term_up.reshape(N_GRP * N_X * N_C, N_ZH, up_rows, 128), ("y", "zl", "x", "c"))
    part_up = part_up.reshape(N_GRP * N_X, N_C, N_ZH, up_rows, 128)
    part_up = jnp.sum(part_up.astype(jnp.float32), axis=0).astype(jnp.bfloat16)
    sum_up = sum_zh(part_up.transpose(1, 0, 2, 3).reshape(N_ZH, N_C * up_rows, 128), zh)

    other = jnp.dot(hidden[rows : rows + fresh_count], down_half, preferred_element_type=jnp.float32)
    mixed = jnp.dot(hidden[:fresh_count], down_half, preferred_element_type=jnp.float32)
    returned = swap(other.astype(jnp.bfloat16)).astype(jnp.float32)
    block_out = (new_rows.astype(jnp.float32) + (mixed + returned)).astype(jnp.bfloat16)

    both = jnp.stack([sum_down, sum_up])
    both = exchange(jnp.broadcast_to(both[None], (N_GRP,) + both.shape), GRP)
    grad_down, grad_up = finish(both, width, hid)
    return (block_out, grad_up, grad_down)


def solution(mesh):
    fine = Mesh(mesh.devices.reshape(tuple(size for _, size in PHYSICAL)), AXES)
    every = P(AXES, None)
    return jax.shard_map(
        body,
        mesh=fine,
        in_specs=(every, P(AXES, None, None), every, every, P(DEV, None), P(DEV, None), P(), every, every),
        out_specs=(every, P(DEV, None), P(DEV, None)),
        check_vma=False,
    )
```

```python
import jax
import jax.numpy as jnp
from jax import lax
from jax.experimental import pallas as pl
from jax.experimental.pallas import tpu as pltpu
from jax.sharding import Mesh, PartitionSpec as P

PHYSICAL = (("y", 4), ("zl", 2), ("zh", 4), ("x", 4), ("c", 2))
SIZE = dict(PHYSICAL)
AXES = tuple(name for name, _ in PHYSICAL)
GRP = ("y", "zl")
DEV = ("zh", "x", "c")
N_GRP = SIZE["y"] * SIZE["zl"]
N_ZH, N_X, N_C = SIZE["zh"], SIZE["x"], SIZE["c"]
VMEM_BYTES = 48 * 1024 * 1024


def normalize(rows, ln_gain):
    values = rows.astype(jnp.float32)
    center = jnp.mean(values, axis=-1, keepdims=True)
    centred = values - center
    spread = jnp.mean(centred * centred, axis=-1, keepdims=True)
    return (centred * lax.rsqrt(spread + 1e-05) * ln_gain.astype(jnp.float32)).astype(jnp.bfloat16)


def swap(value):
    return lax.ppermute(value, "c", [(0, 1), (1, 0)])


def exchange(value, axes):
    return lax.all_to_all(value, axes, split_axis=0, concat_axis=0, tiled=True)


def shift(value, axis, step):
    n = SIZE[axis]
    return lax.ppermute(value, axis, [(i, (i + step) % n) for i in range(n)])


def along(value, axis):
    return [value] + [shift(value, axis, -step) for step in range(1, SIZE[axis])]


def whole(array):
    return pl.BlockSpec(array.shape, lambda *i: (0,) * array.ndim)


def lanes_split(left, right):
    low = lax.broadcasted_iota(jnp.int32, left.shape, 1) < 64
    first = jnp.where(low, left, pltpu.roll(right, 64, 1))
    second = jnp.where(low, pltpu.roll(left, 64, 1), right)
    return first, second


def cut_kernel(at_ref, up_ref, down_ref, out_ref):
    rows = up_ref.shape[0]
    value = up_ref[...].astype(jnp.float32)
    first, second = lanes_split(value[:, :128], value[:, 128:])
    out_ref[:rows, :128] = first.astype(out_ref.dtype)
    out_ref[rows:, :128] = second.astype(out_ref.dtype)
    out_ref[:, 128:] = down_ref[...]


def cut(w_up, w_down, group, y):
    up_rows, down_rows = w_up.shape[0], w_down.shape[0]
    return pl.pallas_call(
        cut_kernel,
        grid_spec=pltpu.PrefetchScalarGridSpec(
            num_scalar_prefetch=1,
            grid=(1,),
            in_specs=[
                pl.BlockSpec((up_rows, 256), lambda i, at: (0, at[0])),
                pl.BlockSpec((down_rows, 256), lambda i, at: (0, at[1])),
            ],
            out_specs=pl.BlockSpec((down_rows, 384), lambda i, at: (0, 0)),
        ),
        out_shape=jax.ShapeDtypeStruct((down_rows, 384), w_up.dtype),
        name="cut",
    )(jnp.stack([group, y]), w_up, w_down)


def spread_kernel(p0, p1, p2, p3, spread_ref, down_ref):
    rows = spread_ref.shape[3]
    for j, part in enumerate((p0, p1, p2, p3)):
        down_ref[j] = part[:, 128:]
        for c in range(N_C):
            value = part[c * rows : (c + 1) * rows, :128]
            for n in range(spread_ref.shape[0]):
                spread_ref[n, c, j] = value


def spread(parts):
    down_rows = parts[0].shape[0]
    rows = down_rows // N_C
    return pl.pallas_call(
        spread_kernel,
        grid=(2,),
        in_specs=[whole(part) for part in parts],
        out_specs=[
            pl.BlockSpec((N_GRP * N_X // 2, N_C, N_ZH, rows, 128), lambda i: (i, 0, 0, 0, 0)),
            pl.BlockSpec((N_ZH, down_rows, 256), lambda i: (0, 0, 0)),
        ],
        out_shape=(
            jax.ShapeDtypeStruct((N_GRP * N_X, N_C, N_ZH, rows, 128), parts[0].dtype),
            jax.ShapeDtypeStruct((N_ZH, down_rows, 256), parts[0].dtype),
        ),
        name="spread",
    )(*parts)


def final_kernel(both_ref, down_ref, up_ref):
    rows = up_ref.shape[0]
    for g in range(N_GRP):
        down_ref[:, g * 128 : (g + 1) * 128] = both_ref[g, 0].astype(jnp.float32)
        left = both_ref[g, 1, :rows].astype(jnp.float32)
        right = both_ref[g, 1, rows:].astype(jnp.float32)
        first, second = lanes_split(left, right)
        up_ref[:, g * 256 : g * 256 + 128] = first
        up_ref[:, g * 256 + 128 : g * 256 + 256] = second


def finish(both, width, hid):
    rows = both.shape[2]
    return pl.pallas_call(
        final_kernel,
        out_shape=(
            jax.ShapeDtypeStruct((rows, width), jnp.float32),
            jax.ShapeDtypeStruct((rows // N_C, hid), jnp.float32),
        ),
        name="finish",
    )(both)


def join_cot(parts, cot):
    at = 0
    for part in parts:
        cot[at : at + part.shape[0], :] = part[...]
        at += part.shape[0]


def forward_kernel(zh_ref, own_ref, partner_ref, c0, c1, w_ref, hidden_ref, pre_ref, cdf_ref, term_ref, w, cot):
    @pl.when(pl.program_id(0) == 0)
    def _():
        join_cot((c0, c1), cot)

    for j in range(N_ZH):
        at = pl.multiple_of(((zh_ref[0] + j) % N_ZH) * 256, 256)
        for g in range(2):
            w[pl.ds(at, 256), g * 128 : (g + 1) * 128] = w_ref[g, :, :, j].reshape(256, 128)
    rows = own_ref.shape[0]
    step = rows // 2
    for which, ref in enumerate((own_ref, partner_ref)):
        for at in range(0, rows, step):
            pre = jnp.dot(ref[at : at + step, :], w[...], preferred_element_type=jnp.float32)
            cdf_value = 0.5 * (1.0 + lax.erf(pre * 0.7071067811865476))
            to = which * rows + at
            hidden_ref[to : to + step, :] = (pre * cdf_value).astype(jnp.bfloat16)
            pre_ref[to : to + step, :] = pre
            cdf_ref[to : to + step, :] = cdf_value.astype(jnp.bfloat16)
    term = lax.dot_general(hidden_ref[...], cot[...], (((0,), (0,)), ((), ())), preferred_element_type=jnp.float32)
    term = term.astype(jnp.bfloat16)
    for x in range(N_X):
        for g in range(N_GRP):
            term_ref[g % 2, x, g // 2, 0] = term[x * 64 : (x + 1) * 64, g * 128 : (g + 1) * 128]


def forward(zh, own, partner, cots, got_up):
    rows, width = own.shape
    half = N_GRP * 128
    return pl.pallas_call(
        forward_kernel,
        grid_spec=pltpu.PrefetchScalarGridSpec(
            num_scalar_prefetch=1,
            grid=(N_ZH,),
            in_specs=[
                whole(own),
                whole(partner),
                *[whole(c) for c in cots],
                pl.BlockSpec((2,) + got_up.shape[1:], lambda q, z: (q, 0, 0, 0, 0, 0)),
            ],
            out_specs=[
                pl.BlockSpec((2 * rows, 256), lambda q, z: (0, q)),
                pl.BlockSpec((2 * rows, 256), lambda q, z: (0, q)),
                pl.BlockSpec((2 * rows, 256), lambda q, z: (0, q)),
                pl.BlockSpec((SIZE["zl"], N_X, SIZE["y"], 1, 64, 128), lambda q, z: (0, 0, 0, q, 0, 0)),
            ],
            scratch_shapes=[pltpu.VMEM((width, 256), jnp.bfloat16), pltpu.VMEM((2 * rows, width), jnp.bfloat16)],
        ),
        out_shape=(
            jax.ShapeDtypeStruct((2 * rows, half), jnp.bfloat16),
            jax.ShapeDtypeStruct((2 * rows, half), jnp.float32),
            jax.ShapeDtypeStruct((2 * rows, half), jnp.bfloat16),
            jax.ShapeDtypeStruct((SIZE["zl"], N_X, SIZE["y"], N_ZH, 64, 128), jnp.bfloat16),
        ),
        compiler_params=pltpu.CompilerParams(vmem_limit_bytes=VMEM_BYTES),
        cost_estimate=pl.CostEstimate(
            flops=0, bytes_accessed=1024, transcendentals=0
        ),
        name="forward",
    )(zh.reshape(1), own, partner, *cots, got_up)


def backward_kernel(at_ref, own_ref, partner_ref, c0, c1, w0, w1, w2, w3, pre_ref, cdf_ref, term_ref, w, pre_grad, cot):
    @pl.when(pl.program_id(0) == 0)
    def _():
        join_cot((c0, c1), cot)

    rows, width = own_ref.shape
    step = rows // 2
    for j, ref in enumerate((w0, w1, w2, w3)):
        column = pl.multiple_of((at_ref[1] + j) % SIZE["y"] * 256, 256)
        for i in range(N_X):
            row = pl.multiple_of((at_ref[2] + i) % N_X * 64, 64)
            w[pl.ds(row, 64), pl.ds(column, 256)] = ref[i, 0]
    for at in range(0, 2 * rows, step):
        back = lax.dot_general(
            cot[at : at + step, :], w[...], (((1,), (1,)), ((), ())), preferred_element_type=jnp.float32
        )
        pre = pre_ref[at : at + step, :]
        density = jnp.exp(-0.5 * pre * pre) * 0.3989422804014327
        slope = cdf_ref[at : at + step, :].astype(jnp.float32) + pre * density
        pre_grad[at : at + step, :] = (back * slope).astype(jnp.bfloat16)
    dims = (((0,), (0,)), ((), ()))
    term = lax.dot_general(own_ref[...], pre_grad[:rows, :], dims, preferred_element_type=jnp.float32)
    term += lax.dot_general(partner_ref[...], pre_grad[rows:, :], dims, preferred_element_type=jnp.float32)
    term = term.astype(jnp.bfloat16)
    for g in range(2):
        for z in range(N_ZH):
            for x in range(N_X):
                for c in range(N_C):
                    at = z * 256 + x * 64 + c * 32
                    term_ref[g, x, c, z] = term[at : at + 32, g * 128 : (g + 1) * 128]


def backward(at, own, partner, cots, downs, pre, cdf_value):
    rows, width = own.shape
    half = N_GRP * 128
    return pl.pallas_call(
        backward_kernel,
        grid_spec=pltpu.PrefetchScalarGridSpec(
            num_scalar_prefetch=1,
            grid=(N_ZH,),
            in_specs=[
                whole(own),
                whole(partner),
                *[whole(c) for c in cots],
                *[pl.BlockSpec((N_X, 1, 64, 256), lambda q, at: (0, (q - at[0] + N_ZH) % N_ZH, 0, 0)) for _ in downs],
                pl.BlockSpec((2 * rows, 256), lambda q, at: (0, q)),
                pl.BlockSpec((2 * rows, 256), lambda q, at: (0, q)),
            ],
            out_specs=[
                pl.BlockSpec((2, N_X, N_C, N_ZH, 32, 128), lambda q, at: (q, 0, 0, 0, 0, 0)),
                pl.BlockSpec((256, width), lambda q, at: (q, 0)),
            ],
            scratch_shapes=[pltpu.VMEM((2 * rows, 256), jnp.bfloat16), pltpu.VMEM((2 * rows, width), jnp.bfloat16)],
        ),
        out_shape=(
            jax.ShapeDtypeStruct((N_GRP, N_X, N_C, N_ZH, 32, 128), jnp.bfloat16),
            jax.ShapeDtypeStruct((half, width), jnp.bfloat16),
        ),
        compiler_params=pltpu.CompilerParams(vmem_limit_bytes=VMEM_BYTES),
        cost_estimate=pl.CostEstimate(
            flops=400 * rows * width * half, bytes_accessed=20 * 1024 * 1024, transcendentals=0
        ),
        name="backward",
    )(at, own, partner, *cots, *downs, pre, cdf_value)


def sum_along(part, axis):
    n, me = SIZE[axis], lax.axis_index(axis)
    total = lax.dynamic_index_in_dim(part, me, 0, keepdims=False).astype(jnp.float32)
    for step in range(1, n):
        block = lax.dynamic_index_in_dim(part, (me + step) % n, 0, keepdims=False)
        total += shift(block, axis, step).astype(jnp.float32)
    return total.astype(jnp.bfloat16)


def body(reservoir, send_rows, send_count, new_rows, w_up, w_down, ln_gain, grad_new, grad_old):
    slots = send_rows.shape[2]
    fresh_count, width = new_rows.shape
    up_rows, hid = w_up.shape
    group, zh = lax.axis_index(GRP), lax.axis_index("zh")

    n_y, n_zl = SIZE["y"], SIZE["zl"]
    y, zl = lax.axis_index("y"), lax.axis_index("zl")
    blocks = grad_old.reshape(n_y, n_zl, slots, width)
    kept = lax.dynamic_index_in_dim(blocks, zl, 1, keepdims=False)
    sent = lax.dynamic_index_in_dim(blocks, 1 - zl, 1, keepdims=False)
    pair = jnp.stack([kept, lax.ppermute(sent, "zl", [(0, 1), (1, 0)])], axis=1)
    parts = along(cut(w_up, w_down, group, y), "zh")
    pair, *parts = lax.optimization_barrier((pair, *parts))
    order, old_cot = [], []
    for dy in range(n_y):
        block = lax.dynamic_index_in_dim(pair, (y + dy) % n_y, 0, keepdims=False)
        if dy:
            block = lax.ppermute(block, "y", [(i, (i + dy) % n_y) for i in range(n_y)])
        old_cot.append(block.reshape(n_zl * slots, width))
        order += [(y - dy) % n_y * n_zl + zl, (y - dy) % n_y * n_zl + 1 - zl]
    order = jnp.stack(order)

    spread_up, down_zh = spread(parts)
    spread_up, *old_cot = lax.optimization_barrier((spread_up, *old_cot))
    cot = jnp.concatenate([grad_new, *old_cot], axis=0)
    spread_up = spread_up.reshape(N_GRP * N_X * N_C, N_ZH, up_rows, 128)
    got_up = exchange(spread_up, ("y", "zl", "x", "c")).reshape(N_GRP, N_X, N_C, N_ZH, up_rows, 128)
    downs = along(jnp.stack(along(down_zh, "x")), "y")

    picks, counts = send_rows[0][order], send_count[0][order]
    live = (lax.broadcasted_iota(jnp.int32, (N_GRP, slots), 1) < counts[:, None]).astype(jnp.bfloat16)
    picked = reservoir[picks.reshape(-1)] * live.reshape(-1, 1)

    normed = normalize(jnp.concatenate([new_rows, picked], axis=0), ln_gain)
    partner = swap(normed)
    cots = (cot, swap(cot))
    rows = normed.shape[0]

    hidden, pre, cdf_value, term_down = forward(zh, normed, partner, cots, got_up)
    part_down = exchange(term_down.reshape((n_zl * N_X,) + term_down.shape[2:]), ("zl", "x"))
    part_down = sum_along(jnp.sum(part_down.astype(jnp.float32), axis=0).astype(jnp.bfloat16), "y")

    at = jnp.stack([zh, y, lax.axis_index("x")])
    term_up, down_half = backward(at, normed, partner, cots, downs, pre, cdf_value)
    part_up = exchange(term_up.reshape(N_GRP * N_X * N_C, N_ZH, up_rows, 128), ("y", "zl", "x", "c"))
    part_up = part_up.reshape(N_GRP * N_X, N_C, N_ZH, up_rows, 128)
    part_up = jnp.sum(part_up.astype(jnp.float32), axis=0).astype(jnp.bfloat16)
    part_up = part_up.transpose(1, 0, 2, 3).reshape(part_down.shape)

    other = jnp.dot(hidden[rows : rows + fresh_count], down_half, preferred_element_type=jnp.float32)
    mixed = jnp.dot(hidden[:fresh_count], down_half, preferred_element_type=jnp.float32)
    returned = swap(other.astype(jnp.bfloat16)).astype(jnp.float32)
    block_out = (new_rows.astype(jnp.float32) + (mixed + returned)).astype(jnp.bfloat16)

    both = sum_along(jnp.stack([part_down, part_up], axis=1), "zh")
    both = exchange(jnp.broadcast_to(both[None], (N_GRP,) + both.shape), GRP)
    grad_down, grad_up = finish(both, width, hid)
    return (block_out, grad_up, grad_down)


def solution(mesh):
    fine = Mesh(mesh.devices.reshape(tuple(size for _, size in PHYSICAL)), AXES)
    every = P(AXES, None)
    return jax.shard_map(
        body,
        mesh=fine,
        in_specs=(every, P(AXES, None, None), every, every, P(DEV, None), P(DEV, None), P(), every, every),
        out_specs=(every, P(DEV, None), P(DEV, None)),
        check_vma=False,
    )
```

```python
import jax
import jax.numpy as jnp
from jax import lax
from jax.experimental import pallas as pl
from jax.experimental.pallas import tpu as pltpu
from jax.sharding import Mesh, PartitionSpec as P

PHYSICAL = (("y", 4), ("zl", 2), ("zh", 4), ("x", 4), ("c", 2))
SIZE = dict(PHYSICAL)
AXES = tuple(name for name, _ in PHYSICAL)
GRP = ("y", "zl")
DEV = ("zh", "x", "c")
N_GRP = SIZE["y"] * SIZE["zl"]
N_ZH, N_X, N_C = SIZE["zh"], SIZE["x"], SIZE["c"]
VMEM_BYTES = 48 * 1024 * 1024


def normalize(rows, ln_gain):
    values = rows.astype(jnp.float32)
    center = jnp.mean(values, axis=-1, keepdims=True)
    centred = values - center
    spread = jnp.mean(centred * centred, axis=-1, keepdims=True)
    return (centred * lax.rsqrt(spread + 1e-05) * ln_gain.astype(jnp.float32)).astype(jnp.bfloat16)


def swap(value):
    return lax.ppermute(value, "c", [(0, 1), (1, 0)])


def exchange(value, axes):
    return lax.all_to_all(value, axes, split_axis=0, concat_axis=0, tiled=True)


def shift(value, axis, step):
    n = SIZE[axis]
    return lax.ppermute(value, axis, [(i, (i + step) % n) for i in range(n)])


def along(value, axis):
    return [value] + [shift(value, axis, -step) for step in range(1, SIZE[axis])]


def whole(array):
    return pl.BlockSpec(array.shape, lambda *i: (0,) * array.ndim)


def lanes_split(left, right):
    low = lax.broadcasted_iota(jnp.int32, left.shape, 1) < 64
    first = jnp.where(low, left, pltpu.roll(right, 64, 1))
    second = jnp.where(low, pltpu.roll(left, 64, 1), right)
    return first, second


def cut_kernel(at_ref, up_ref, down_ref, out_ref):
    rows = up_ref.shape[0]
    value = up_ref[...].astype(jnp.float32)
    first, second = lanes_split(value[:, :128], value[:, 128:])
    out_ref[:rows, :128] = first.astype(out_ref.dtype)
    out_ref[rows:, :128] = second.astype(out_ref.dtype)
    out_ref[:, 128:] = down_ref[...]


def cut(w_up, w_down, group, y):
    up_rows, down_rows = w_up.shape[0], w_down.shape[0]
    return pl.pallas_call(
        cut_kernel,
        grid_spec=pltpu.PrefetchScalarGridSpec(
            num_scalar_prefetch=1,
            grid=(1,),
            in_specs=[
                pl.BlockSpec((up_rows, 256), lambda i, at: (0, at[0])),
                pl.BlockSpec((down_rows, 256), lambda i, at: (0, at[1])),
            ],
            out_specs=pl.BlockSpec((down_rows, 384), lambda i, at: (0, 0)),
        ),
        out_shape=jax.ShapeDtypeStruct((down_rows, 384), w_up.dtype),
        name="cut",
    )(jnp.stack([group, y]), w_up, w_down)


def spread_kernel(p0, p1, p2, p3, spread_ref, down_ref):
    rows = spread_ref.shape[3]
    for j, part in enumerate((p0, p1, p2, p3)):
        down_ref[:, j * 256 : (j + 1) * 256] = part[:, 128:]
        for c in range(N_C):
            value = part[c * rows : (c + 1) * rows, :128]
            for n in range(spread_ref.shape[0]):
                spread_ref[n, c, j] = value


def spread(parts):
    down_rows = parts[0].shape[0]
    rows = down_rows // N_C
    return pl.pallas_call(
        spread_kernel,
        grid=(2,),
        in_specs=[whole(part) for part in parts],
        out_specs=[
            pl.BlockSpec((N_GRP * N_X // 2, N_C, N_ZH, rows, 128), lambda i: (i, 0, 0, 0, 0)),
            pl.BlockSpec((down_rows, N_ZH * 256), lambda i: (0, 0)),
        ],
        out_shape=(
            jax.ShapeDtypeStruct((N_GRP * N_X, N_C, N_ZH, rows, 128), parts[0].dtype),
            jax.ShapeDtypeStruct((down_rows, N_ZH * 256), parts[0].dtype),
        ),
        name="spread",
    )(*parts)


def final_kernel(both_ref, down_ref, up_ref):
    rows = up_ref.shape[0]
    for g in range(N_GRP):
        down_ref[:, g * 128 : (g + 1) * 128] = both_ref[g, 0].astype(jnp.float32)
        left = both_ref[g, 1, :rows].astype(jnp.float32)
        right = both_ref[g, 1, rows:].astype(jnp.float32)
        first, second = lanes_split(left, right)
        up_ref[:, g * 256 : g * 256 + 128] = first
        up_ref[:, g * 256 + 128 : g * 256 + 256] = second


def finish(both, width, hid):
    rows = both.shape[2]
    return pl.pallas_call(
        final_kernel,
        out_shape=(
            jax.ShapeDtypeStruct((rows, width), jnp.float32),
            jax.ShapeDtypeStruct((rows // N_C, hid), jnp.float32),
        ),
        name="finish",
    )(both)


def join_cot(parts, cot):
    at = 0
    for part in parts:
        cot[at : at + part.shape[0], :] = part[...]
        at += part.shape[0]


def forward_kernel(zh_ref, own_ref, partner_ref, c0, c1, w_ref, hidden_ref, pre_ref, cdf_ref, term_ref, w, cot):
    @pl.when(pl.program_id(0) == 0)
    def _():
        join_cot((c0, c1), cot)

    for j in range(N_ZH):
        at = pl.multiple_of(((zh_ref[0] + j) % N_ZH) * 256, 256)
        for g in range(2):
            w[pl.ds(at, 256), g * 128 : (g + 1) * 128] = w_ref[g, :, :, j].reshape(256, 128)
    rows = own_ref.shape[0]
    step = rows // 2
    for which, ref in enumerate((own_ref, partner_ref)):
        for at in range(0, rows, step):
            pre = jnp.dot(ref[at : at + step, :], w[...], preferred_element_type=jnp.float32)
            cdf_value = 0.5 * (1.0 + lax.erf(pre * 0.7071067811865476))
            to = which * rows + at
            hidden_ref[to : to + step, :] = (pre * cdf_value).astype(jnp.bfloat16)
            pre_ref[to : to + step, :] = pre
            cdf_ref[to : to + step, :] = cdf_value.astype(jnp.bfloat16)
    term = lax.dot_general(hidden_ref[...], cot[...], (((0,), (0,)), ((), ())), preferred_element_type=jnp.float32)
    term = term.astype(jnp.bfloat16)
    for x in range(N_X):
        for g in range(N_GRP):
            term_ref[g, x, 0] = term[x * 64 : (x + 1) * 64, g * 128 : (g + 1) * 128]


def forward(zh, own, partner, cots, got_up):
    rows, width = own.shape
    half = N_GRP * 128
    return pl.pallas_call(
        forward_kernel,
        grid_spec=pltpu.PrefetchScalarGridSpec(
            num_scalar_prefetch=1,
            grid=(N_ZH,),
            in_specs=[
                whole(own),
                whole(partner),
                *[whole(c) for c in cots],
                pl.BlockSpec((2,) + got_up.shape[1:], lambda q, z: (q, 0, 0, 0, 0, 0)),
            ],
            out_specs=[
                pl.BlockSpec((2 * rows, 256), lambda q, z: (0, q)),
                pl.BlockSpec((2 * rows, 256), lambda q, z: (0, q)),
                pl.BlockSpec((2 * rows, 256), lambda q, z: (0, q)),
                pl.BlockSpec((N_GRP, N_X, 1, 64, 128), lambda q, z: (0, 0, q, 0, 0)),
            ],
            scratch_shapes=[pltpu.VMEM((width, 256), jnp.bfloat16), pltpu.VMEM((2 * rows, width), jnp.bfloat16)],
        ),
        out_shape=(
            jax.ShapeDtypeStruct((2 * rows, half), jnp.bfloat16),
            jax.ShapeDtypeStruct((2 * rows, half), jnp.float32),
            jax.ShapeDtypeStruct((2 * rows, half), jnp.bfloat16),
            jax.ShapeDtypeStruct((N_GRP, N_X, N_ZH, 64, 128), jnp.bfloat16),
        ),
        compiler_params=pltpu.CompilerParams(vmem_limit_bytes=VMEM_BYTES),
        cost_estimate=pl.CostEstimate(
            flops=0, bytes_accessed=1024, transcendentals=0
        ),
        name="forward",
    )(zh.reshape(1), own, partner, *cots, got_up)


def backward_kernel(at_ref, own_ref, partner_ref, c0, c1, w0, w1, w2, w3, pre_ref, cdf_ref, term_ref, w, pre_grad, cot):
    @pl.when(pl.program_id(0) == 0)
    def _():
        join_cot((c0, c1), cot)

    rows, width = own_ref.shape
    step = rows // 2
    for j, ref in enumerate((w0, w1, w2, w3)):
        row = pl.multiple_of((at_ref[2] + j) % N_X * 64, 64)
        for i in range(SIZE["y"]):
            column = pl.multiple_of((at_ref[1] + SIZE["y"] - i) % SIZE["y"] * 256, 256)
            w[pl.ds(row, 64), pl.ds(column, 256)] = ref[i]
    for at in range(0, 2 * rows, step):
        back = lax.dot_general(
            cot[at : at + step, :], w[...], (((1,), (1,)), ((), ())), preferred_element_type=jnp.float32
        )
        pre = pre_ref[at : at + step, :]
        density = jnp.exp(-0.5 * pre * pre) * 0.3989422804014327
        slope = cdf_ref[at : at + step, :].astype(jnp.float32) + pre * density
        pre_grad[at : at + step, :] = (back * slope).astype(jnp.bfloat16)
    dims = (((0,), (0,)), ((), ()))
    term = lax.dot_general(own_ref[...], pre_grad[:rows, :], dims, preferred_element_type=jnp.float32)
    term += lax.dot_general(partner_ref[...], pre_grad[rows:, :], dims, preferred_element_type=jnp.float32)
    term = term.astype(jnp.bfloat16)
    for g in range(2):
        for z in range(N_ZH):
            for x in range(N_X):
                for c in range(N_C):
                    at = z * 256 + x * 64 + c * 32
                    term_ref[g, x, c, z] = term[at : at + 32, g * 128 : (g + 1) * 128]


def backward(at, own, partner, cots, downs, pre, cdf_value):
    rows, width = own.shape
    half = N_GRP * 128
    return pl.pallas_call(
        backward_kernel,
        grid_spec=pltpu.PrefetchScalarGridSpec(
            num_scalar_prefetch=1,
            grid=(N_ZH,),
            in_specs=[
                whole(own),
                whole(partner),
                *[whole(c) for c in cots],
                *[pl.BlockSpec((SIZE["y"], 64, 256), lambda q, at: (0, 0, (q - at[0] + N_ZH) % N_ZH)) for _ in downs],
                pl.BlockSpec((2 * rows, 256), lambda q, at: (0, q)),
                pl.BlockSpec((2 * rows, 256), lambda q, at: (0, q)),
            ],
            out_specs=[
                pl.BlockSpec((2, N_X, N_C, N_ZH, 32, 128), lambda q, at: (q, 0, 0, 0, 0, 0)),
                pl.BlockSpec((256, width), lambda q, at: (q, 0)),
            ],
            scratch_shapes=[pltpu.VMEM((2 * rows, 256), jnp.bfloat16), pltpu.VMEM((2 * rows, width), jnp.bfloat16)],
        ),
        out_shape=(
            jax.ShapeDtypeStruct((N_GRP, N_X, N_C, N_ZH, 32, 128), jnp.bfloat16),
            jax.ShapeDtypeStruct((half, width), jnp.bfloat16),
        ),
        compiler_params=pltpu.CompilerParams(vmem_limit_bytes=VMEM_BYTES),
        cost_estimate=pl.CostEstimate(
            flops=400 * rows * width * half, bytes_accessed=20 * 1024 * 1024, transcendentals=0
        ),
        name="backward",
    )(at, own, partner, *cots, *downs, pre, cdf_value)


def sum_along(part, axis):
    n, me = SIZE[axis], lax.axis_index(axis)
    total = lax.dynamic_index_in_dim(part, me, 0, keepdims=False).astype(jnp.float32)
    for step in range(1, n):
        block = lax.dynamic_index_in_dim(part, (me + step) % n, 0, keepdims=False)
        total += shift(block, axis, step).astype(jnp.float32)
    return total.astype(jnp.bfloat16)


def body(reservoir, send_rows, send_count, new_rows, w_up, w_down, ln_gain, grad_new, grad_old):
    slots = send_rows.shape[2]
    fresh_count, width = new_rows.shape
    up_rows, hid = w_up.shape
    group, zh = lax.axis_index(GRP), lax.axis_index("zh")

    n_y, n_zl = SIZE["y"], SIZE["zl"]
    y, zl = lax.axis_index("y"), lax.axis_index("zl")
    blocks = grad_old.reshape(n_y, n_zl, slots, width)
    kept = lax.dynamic_index_in_dim(blocks, zl, 1, keepdims=False)
    sent = lax.dynamic_index_in_dim(blocks, 1 - zl, 1, keepdims=False)
    pair = jnp.stack([kept, lax.ppermute(sent, "zl", [(0, 1), (1, 0)])], axis=1)
    parts = along(cut(w_up, w_down, group, y), "zh")
    pair, *parts = lax.optimization_barrier((pair, *parts))
    spread_up, down_zh = spread(parts)
    spread_up = spread_up.reshape(N_GRP * N_X * N_C, N_ZH, up_rows, 128)
    old_rows = n_zl * slots
    order, old_cot, down_y = [], [], []
    for dy in range(n_y):
        block = lax.dynamic_index_in_dim(pair, (y + dy) % n_y, 0, keepdims=False).reshape(old_rows, width)
        if dy:
            block = shift(jnp.concatenate([block, down_zh], axis=0), "y", dy)
        old_cot.append(block[:old_rows])
        down_y.append(block[old_rows:] if dy else down_zh)
        order += [(y - dy) % n_y * n_zl + zl, (y - dy) % n_y * n_zl + 1 - zl]
    order = jnp.stack(order)
    spread_up, *old_cot = lax.optimization_barrier((spread_up, *old_cot))
    cot = jnp.concatenate([grad_new, *old_cot], axis=0)
    got_up = exchange(spread_up, ("y", "zl", "x", "c")).reshape(N_GRP, N_X, N_C, N_ZH, up_rows, 128)
    downs = along(jnp.stack(down_y), "x")

    picks, counts = send_rows[0][order], send_count[0][order]
    live = (lax.broadcasted_iota(jnp.int32, (N_GRP, slots), 1) < counts[:, None]).astype(jnp.bfloat16)
    picked = reservoir[picks.reshape(-1)] * live.reshape(-1, 1)

    normed = normalize(jnp.concatenate([new_rows, picked], axis=0), ln_gain)
    partner = swap(normed)
    cots = (cot, swap(cot))
    rows = normed.shape[0]

    hidden, pre, cdf_value, term_down = forward(zh, normed, partner, cots, got_up)
    part_down = exchange(term_down, GRP)
    part_down = sum_along(jnp.sum(part_down.astype(jnp.float32), axis=0).astype(jnp.bfloat16), "x")

    at = jnp.stack([zh, y, lax.axis_index("x")])
    term_up, down_half = backward(at, normed, partner, cots, downs, pre, cdf_value)
    part_up = exchange(term_up.reshape(N_GRP * N_X * N_C, N_ZH, up_rows, 128), ("y", "zl", "x", "c"))
    part_up = part_up.reshape(N_GRP * N_X, N_C, N_ZH, up_rows, 128)
    part_up = jnp.sum(part_up.astype(jnp.float32), axis=0).astype(jnp.bfloat16)
    part_up = part_up.transpose(1, 0, 2, 3).reshape(part_down.shape)

    other = jnp.dot(hidden[rows : rows + fresh_count], down_half, preferred_element_type=jnp.float32)
    mixed = jnp.dot(hidden[:fresh_count], down_half, preferred_element_type=jnp.float32)
    returned = swap(other.astype(jnp.bfloat16)).astype(jnp.float32)
    block_out = (new_rows.astype(jnp.float32) + (mixed + returned)).astype(jnp.bfloat16)

    both = sum_along(jnp.stack([part_down, part_up], axis=1), "zh")
    both = exchange(jnp.broadcast_to(both[None], (N_GRP,) + both.shape), GRP)
    grad_down, grad_up = finish(both, width, hid)
    return (block_out, grad_up, grad_down)


def solution(mesh):
    fine = Mesh(mesh.devices.reshape(tuple(size for _, size in PHYSICAL)), AXES)
    every = P(AXES, None)
    return jax.shard_map(
        body,
        mesh=fine,
        in_specs=(every, P(AXES, None, None), every, every, P(DEV, None), P(DEV, None), P(), every, every),
        out_specs=(every, P(DEV, None), P(DEV, None)),
        check_vma=False,
    )
```

```python
import jax
import jax.numpy as jnp
from jax import lax
from jax.experimental import pallas as pl
from jax.experimental.pallas import tpu as pltpu
from jax.sharding import Mesh, PartitionSpec as P

PHYSICAL = (("y", 4), ("zl", 2), ("zh", 4), ("x", 4), ("c", 2))
SIZE = dict(PHYSICAL)
AXES = tuple(name for name, _ in PHYSICAL)
GRP = ("y", "zl")
DEV = ("zh", "x", "c")
N_GRP = SIZE["y"] * SIZE["zl"]
N_ZH, N_X, N_C = SIZE["zh"], SIZE["x"], SIZE["c"]
VMEM_BYTES = 48 * 1024 * 1024


def normalize(rows, ln_gain):
    values = rows.astype(jnp.float32)
    center = jnp.mean(values, axis=-1, keepdims=True)
    centred = values - center
    spread = jnp.mean(centred * centred, axis=-1, keepdims=True)
    return (centred * lax.rsqrt(spread + 1e-05) * ln_gain.astype(jnp.float32)).astype(jnp.bfloat16)


def swap(value):
    return lax.ppermute(value, "c", [(0, 1), (1, 0)])


def exchange(value, axes):
    return lax.all_to_all(value, axes, split_axis=0, concat_axis=0, tiled=True)


def shift(value, axis, step):
    n = SIZE[axis]
    return lax.ppermute(value, axis, [(i, (i + step) % n) for i in range(n)])


def along(value, axis):
    return [value] + [shift(value, axis, -step) for step in range(1, SIZE[axis])]


def whole(array):
    return pl.BlockSpec(array.shape, lambda *i: (0,) * array.ndim)


def lanes_split(left, right):
    low = lax.broadcasted_iota(jnp.int32, left.shape, 1) < 64
    first = jnp.where(low, left, pltpu.roll(right, 64, 1))
    second = jnp.where(low, pltpu.roll(left, 64, 1), right)
    return first, second


def cut_kernel(at_ref, up_ref, down_ref, out_ref):
    rows = up_ref.shape[0]
    value = up_ref[...].astype(jnp.float32)
    first, second = lanes_split(value[:, :128], value[:, 128:])
    out_ref[:rows, :128] = first.astype(out_ref.dtype)
    out_ref[rows:, :128] = second.astype(out_ref.dtype)
    out_ref[:, 128:] = down_ref[...]


def cut(w_up, w_down, group, y):
    up_rows, down_rows = w_up.shape[0], w_down.shape[0]
    return pl.pallas_call(
        cut_kernel,
        grid_spec=pltpu.PrefetchScalarGridSpec(
            num_scalar_prefetch=1,
            grid=(1,),
            in_specs=[
                pl.BlockSpec((up_rows, 256), lambda i, at: (0, at[0])),
                pl.BlockSpec((down_rows, 256), lambda i, at: (0, at[1])),
            ],
            out_specs=pl.BlockSpec((down_rows, 384), lambda i, at: (0, 0)),
        ),
        out_shape=jax.ShapeDtypeStruct((down_rows, 384), w_up.dtype),
        name="cut",
    )(jnp.stack([group, y]), w_up, w_down)


def spread_kernel(p0, p1, p2, p3, spread_ref, down_ref):
    rows = spread_ref.shape[3]
    for j, part in enumerate((p0, p1, p2, p3)):
        down_ref[:, j * 256 : (j + 1) * 256] = part[:, 128:]
        for c in range(N_C):
            value = part[c * rows : (c + 1) * rows, :128]
            for n in range(spread_ref.shape[0]):
                spread_ref[n, c, j] = value


def spread(parts):
    down_rows = parts[0].shape[0]
    rows = down_rows // N_C
    return pl.pallas_call(
        spread_kernel,
        grid=(2,),
        in_specs=[whole(part) for part in parts],
        out_specs=[
            pl.BlockSpec((N_GRP * N_X // 2, N_C, N_ZH, rows, 128), lambda i: (i, 0, 0, 0, 0)),
            pl.BlockSpec((down_rows, N_ZH * 256), lambda i: (0, 0)),
        ],
        out_shape=(
            jax.ShapeDtypeStruct((N_GRP * N_X, N_C, N_ZH, rows, 128), parts[0].dtype),
            jax.ShapeDtypeStruct((down_rows, N_ZH * 256), parts[0].dtype),
        ),
        name="spread",
    )(*parts)


def final_kernel(both_ref, down_ref, up_ref):
    rows = up_ref.shape[0]
    for g in range(N_GRP):
        down_ref[:, g * 128 : (g + 1) * 128] = both_ref[g, 0].astype(jnp.float32)
        left = both_ref[g, 1, :rows].astype(jnp.float32)
        right = both_ref[g, 1, rows:].astype(jnp.float32)
        first, second = lanes_split(left, right)
        up_ref[:, g * 256 : g * 256 + 128] = first
        up_ref[:, g * 256 + 128 : g * 256 + 256] = second


def finish(both, width, hid):
    rows = both.shape[2]
    return pl.pallas_call(
        final_kernel,
        out_shape=(
            jax.ShapeDtypeStruct((rows, width), jnp.float32),
            jax.ShapeDtypeStruct((rows // N_C, hid), jnp.float32),
        ),
        name="finish",
    )(both)


def join_cot(parts, cot):
    at = 0
    for part in parts:
        cot[at : at + part.shape[0], :] = part[...]
        at += part.shape[0]


def forward_kernel(zh_ref, own_ref, partner_ref, c0, c1, w_ref, hidden_ref, pre_ref, cdf_ref, term_ref, w, cot):
    @pl.when(pl.program_id(0) == 0)
    def _():
        join_cot((c0, c1), cot)

    for j in range(N_ZH):
        at = pl.multiple_of(((zh_ref[0] + j) % N_ZH) * 256, 256)
        for g in range(2):
            w[pl.ds(at, 256), g * 128 : (g + 1) * 128] = w_ref[g, :, :, j].reshape(256, 128)
    rows = own_ref.shape[0]
    step = rows // 2
    for which, ref in enumerate((own_ref, partner_ref)):
        for at in range(0, rows, step):
            pre = jnp.dot(ref[at : at + step, :], w[...], preferred_element_type=jnp.float32)
            cdf_value = 0.5 * (1.0 + lax.erf(pre * 0.7071067811865476))
            to = which * rows + at
            hidden_ref[to : to + step, :] = (pre * cdf_value).astype(jnp.bfloat16)
            pre_ref[to : to + step, :] = pre
            cdf_ref[to : to + step, :] = cdf_value.astype(jnp.bfloat16)
    term = lax.dot_general(hidden_ref[...], cot[...], (((0,), (0,)), ((), ())), preferred_element_type=jnp.float32)
    term = term.astype(jnp.bfloat16)
    for x in range(N_X):
        for g in range(N_GRP):
            term_ref[g, x, 0] = term[x * 64 : (x + 1) * 64, g * 128 : (g + 1) * 128]


def forward(zh, own, partner, cots, got_up):
    rows, width = own.shape
    half = N_GRP * 128
    return pl.pallas_call(
        forward_kernel,
        grid_spec=pltpu.PrefetchScalarGridSpec(
            num_scalar_prefetch=1,
            grid=(N_ZH,),
            in_specs=[
                whole(own),
                whole(partner),
                *[whole(c) for c in cots],
                pl.BlockSpec((2,) + got_up.shape[1:], lambda q, z: (q, 0, 0, 0, 0, 0)),
            ],
            out_specs=[
                pl.BlockSpec((2 * rows, 256), lambda q, z: (0, q)),
                pl.BlockSpec((2 * rows, 256), lambda q, z: (0, q)),
                pl.BlockSpec((2 * rows, 256), lambda q, z: (0, q)),
                pl.BlockSpec((N_GRP, N_X, 1, 64, 128), lambda q, z: (0, 0, q, 0, 0)),
            ],
            scratch_shapes=[pltpu.VMEM((width, 256), jnp.bfloat16), pltpu.VMEM((2 * rows, width), jnp.bfloat16)],
        ),
        out_shape=(
            jax.ShapeDtypeStruct((2 * rows, half), jnp.bfloat16),
            jax.ShapeDtypeStruct((2 * rows, half), jnp.float32),
            jax.ShapeDtypeStruct((2 * rows, half), jnp.bfloat16),
            jax.ShapeDtypeStruct((N_GRP, N_X, N_ZH, 64, 128), jnp.bfloat16),
        ),
        compiler_params=pltpu.CompilerParams(vmem_limit_bytes=VMEM_BYTES),
        cost_estimate=pl.CostEstimate(
            flops=0, bytes_accessed=1024, transcendentals=0
        ),
        name="forward",
    )(zh.reshape(1), own, partner, *cots, got_up)


def backward_kernel(at_ref, own_ref, partner_ref, c0, c1, w0, w1, w2, w3, pre_ref, cdf_ref, term_ref, w, pre_grad, cot):
    @pl.when(pl.program_id(0) == 0)
    def _():
        join_cot((c0, c1), cot)

    rows, width = own_ref.shape
    step = rows // 2
    for j, ref in enumerate((w0, w1, w2, w3)):
        row = pl.multiple_of((at_ref[2] + j) % N_X * 64, 64)
        for i in range(SIZE["y"]):
            column = pl.multiple_of((at_ref[1] + SIZE["y"] - i) % SIZE["y"] * 256, 256)
            w[pl.ds(row, 64), pl.ds(column, 256)] = ref[i]
    for at in range(0, 2 * rows, step):
        back = lax.dot_general(
            cot[at : at + step, :], w[...], (((1,), (1,)), ((), ())), preferred_element_type=jnp.float32
        )
        pre = pre_ref[at : at + step, :]
        density = jnp.exp(-0.5 * pre * pre) * 0.3989422804014327
        slope = cdf_ref[at : at + step, :].astype(jnp.float32) + pre * density
        pre_grad[at : at + step, :] = (back * slope).astype(jnp.bfloat16)
    dims = (((0,), (0,)), ((), ()))
    term = lax.dot_general(own_ref[...], pre_grad[:rows, :], dims, preferred_element_type=jnp.float32)
    term += lax.dot_general(partner_ref[...], pre_grad[rows:, :], dims, preferred_element_type=jnp.float32)
    term = term.astype(jnp.bfloat16)
    for g in range(2):
        for z in range(N_ZH):
            for x in range(N_X):
                for c in range(N_C):
                    at = z * 256 + x * 64 + c * 32
                    term_ref[g, x, c, z] = term[at : at + 32, g * 128 : (g + 1) * 128]


def backward(at, own, partner, cots, downs, pre, cdf_value):
    rows, width = own.shape
    half = N_GRP * 128
    return pl.pallas_call(
        backward_kernel,
        grid_spec=pltpu.PrefetchScalarGridSpec(
            num_scalar_prefetch=1,
            grid=(N_ZH,),
            in_specs=[
                whole(own),
                whole(partner),
                *[whole(c) for c in cots],
                *[pl.BlockSpec((SIZE["y"], 64, 256), lambda q, at: (0, 0, (q - at[0] + N_ZH) % N_ZH)) for _ in downs],
                pl.BlockSpec((2 * rows, 256), lambda q, at: (0, q)),
                pl.BlockSpec((2 * rows, 256), lambda q, at: (0, q)),
            ],
            out_specs=[
                pl.BlockSpec((2, N_X, N_C, N_ZH, 32, 128), lambda q, at: (q, 0, 0, 0, 0, 0)),
                pl.BlockSpec((256, width), lambda q, at: (q, 0)),
            ],
            scratch_shapes=[pltpu.VMEM((2 * rows, 256), jnp.bfloat16), pltpu.VMEM((2 * rows, width), jnp.bfloat16)],
        ),
        out_shape=(
            jax.ShapeDtypeStruct((N_GRP, N_X, N_C, N_ZH, 32, 128), jnp.bfloat16),
            jax.ShapeDtypeStruct((half, width), jnp.bfloat16),
        ),
        compiler_params=pltpu.CompilerParams(vmem_limit_bytes=VMEM_BYTES),
        cost_estimate=pl.CostEstimate(
            flops=400 * rows * width * half, bytes_accessed=20 * 1024 * 1024, transcendentals=0
        ),
        name="backward",
    )(at, own, partner, *cots, *downs, pre, cdf_value)


def sum_along(part, axis):
    n, me = SIZE[axis], lax.axis_index(axis)
    total = lax.dynamic_index_in_dim(part, me, 0, keepdims=False).astype(jnp.float32)
    for step in range(1, n):
        block = lax.dynamic_index_in_dim(part, (me + step) % n, 0, keepdims=False)
        total += shift(block, axis, step).astype(jnp.float32)
    return total.astype(jnp.bfloat16)


def body(reservoir, send_rows, send_count, new_rows, w_up, w_down, ln_gain, grad_new, grad_old):
    slots = send_rows.shape[2]
    fresh_count, width = new_rows.shape
    up_rows, hid = w_up.shape
    group, zh = lax.axis_index(GRP), lax.axis_index("zh")

    n_y, n_zl = SIZE["y"], SIZE["zl"]
    y, zl = lax.axis_index("y"), lax.axis_index("zl")
    blocks = grad_old.reshape(n_y, n_zl, slots, width)
    kept = lax.dynamic_index_in_dim(blocks, zl, 1, keepdims=False)
    sent = lax.dynamic_index_in_dim(blocks, 1 - zl, 1, keepdims=False)
    pair = jnp.stack([kept, lax.ppermute(sent, "zl", [(0, 1), (1, 0)])], axis=1)
    parts = along(cut(w_up, w_down, group, y), "zh")
    pair, *parts = lax.optimization_barrier((pair, *parts))
    spread_up, down_zh = spread(parts)
    spread_up = spread_up.reshape(N_GRP * N_X * N_C, N_ZH, up_rows, 128)
    old_rows = n_zl * slots
    order, old_cot, down_y = [], [], []
    for dy in range(n_y):
        block = lax.dynamic_index_in_dim(pair, (y + dy) % n_y, 0, keepdims=False).reshape(old_rows, width)
        if dy:
            block = shift(jnp.concatenate([block, down_zh], axis=0), "y", dy)
        old_cot.append(block[:old_rows])
        down_y.append(block[old_rows:] if dy else down_zh)
        order += [(y - dy) % n_y * n_zl + zl, (y - dy) % n_y * n_zl + 1 - zl]
    order = jnp.stack(order)
    cot = jnp.concatenate([grad_new, *old_cot], axis=0)
    got_up = exchange(spread_up, ("y", "zl", "x", "c")).reshape(N_GRP, N_X, N_C, N_ZH, up_rows, 128)
    downs = along(jnp.stack(down_y), "x")

    picks, counts = send_rows[0][order], send_count[0][order]
    live = (lax.broadcasted_iota(jnp.int32, (N_GRP, slots), 1) < counts[:, None]).astype(jnp.bfloat16)
    picked = reservoir[picks.reshape(-1)] * live.reshape(-1, 1)

    normed = normalize(jnp.concatenate([new_rows, picked], axis=0), ln_gain)
    partner = swap(normed)
    cots = (cot, swap(cot))
    rows = normed.shape[0]

    hidden, pre, cdf_value, term_down = forward(zh, normed, partner, cots, got_up)
    part_down = exchange(term_down, GRP)
    part_down = sum_along(jnp.sum(part_down.astype(jnp.float32), axis=0).astype(jnp.bfloat16), "x")

    at = jnp.stack([zh, y, lax.axis_index("x")])
    term_up, down_half = backward(at, normed, partner, cots, downs, pre, cdf_value)
    part_up = exchange(term_up.reshape(N_GRP * N_X * N_C, N_ZH, up_rows, 128), ("y", "zl", "x", "c"))
    part_up = part_up.reshape(N_GRP * N_X, N_C, N_ZH, up_rows, 128)
    part_up = jnp.sum(part_up.astype(jnp.float32), axis=0).astype(jnp.bfloat16)
    part_up = part_up.transpose(1, 0, 2, 3).reshape(part_down.shape)

    other = jnp.dot(hidden[rows : rows + fresh_count], down_half, preferred_element_type=jnp.float32)
    mixed = jnp.dot(hidden[:fresh_count], down_half, preferred_element_type=jnp.float32)
    returned = swap(other.astype(jnp.bfloat16)).astype(jnp.float32)
    block_out = (new_rows.astype(jnp.float32) + (mixed + returned)).astype(jnp.bfloat16)

    both = sum_along(jnp.stack([part_down, part_up], axis=1), "zh")
    both = exchange(jnp.broadcast_to(both[None], (N_GRP,) + both.shape), GRP)
    grad_down, grad_up = finish(both, width, hid)
    return (block_out, grad_up, grad_down)


def solution(mesh):
    fine = Mesh(mesh.devices.reshape(tuple(size for _, size in PHYSICAL)), AXES)
    every = P(AXES, None)
    return jax.shard_map(
        body,
        mesh=fine,
        in_specs=(every, P(AXES, None, None), every, every, P(DEV, None), P(DEV, None), P(), every, every),
        out_specs=(every, P(DEV, None), P(DEV, None)),
        check_vma=False,
    )
```
